512 devices in a mesh: dp: 64 (over x_lo, z, core), tensor: 8 (over x_hi, y).
Axes of the slice: x: 4 (x_hi: 2, x_lo: 2; x = x_hi * 2 + x_lo), y: 4, z: 16, core: 2. Of those that a mesh axis runs over, the one named last changes fastest.
Arguments:
- tokens: bfloat16 [16384, 8192], P('dp', 'tensor'), may hold values from -6 to 6
- cotangent: bfloat16 [16384, 8192], P('dp', 'tensor'), may hold values from -6 to 6
- gate_inner: bfloat16 [64, 128, 128], P('tensor', 'dp'), may hold values from -0.5 to 0.5
- gate_outer: bfloat16 [64, 128, 128], P('tensor', 'dp'), may hold values from -0.5 to 0.5
- value_inner: bfloat16 [64, 128, 128], P('tensor', 'dp'), may hold values from -0.5 to 0.5
- value_outer: bfloat16 [64, 128, 128], P('tensor', 'dp'), may hold values from -0.5 to 0.5
- down_inner: bfloat16 [64, 128, 128], P('tensor', 'dp'), may hold values from -0.5 to 0.5
- down_outer: bfloat16 [64, 128, 128], P('tensor', 'dp'), may hold values from -0.5 to 0.5
Outputs:
- mixed: bfloat16 [16384, 8192], P('dp', 'tensor')
- tokens_grad: bfloat16 [16384, 8192], P('dp', 'tensor')
- gate_inner_grad: float32 [64, 128, 128], P('tensor', 'dp')
- gate_outer_grad: float32 [64, 128, 128], P('tensor', 'dp')
- value_inner_grad: float32 [64, 128, 128], P('tensor', 'dp')
- value_outer_grad: float32 [64, 128, 128], P('tensor', 'dp')
- down_inner_grad: float32 [64, 128, 128], P('tensor', 'dp')
- down_outer_grad: float32 [64, 128, 128], P('tensor', 'dp')
The draws below stay inside these ranges and needn't reach their ends.
All inputs are finite; a program needn't handle non-finite values.
Results may differ from the reference program's by a relative error of at most 0.0072.
Values may be sent and summed in bfloat16 or wider, within the bound.
No kernel may reach another device: no remote copies, remote signals or barrier semaphores. Data moves between devices by JAX's collectives and lax.ppermute only.
A program may use at most 64 MiB of HBM per device.

```python
import jax
import jax.numpy as jnp
from jax import lax

NB = 64
BS = 128
D = 8192
TOK_DEV = 256
TOKENS = 16384
N_DP = 64


def level_of(stream_key, extent, shards, low, top_value):
    gain = 1.0
    for axis_at, parts in shards:
        steps = jax.random.uniform(jax.random.fold_in(jax.random.fold_in(stream_key, 6), axis_at), (parts,), jnp.float32, low / len(shards), top_value / len(shards))
        gain = gain * jnp.repeat(jnp.exp(steps), extent[axis_at] // parts).reshape((-1,) + (1,) * (len(extent) - 1 - axis_at))
    return gain


def scatter_about(rng, extent, scale, bound, cuts=(), kind=jnp.bfloat16):
    values = scale * jax.random.normal(rng, extent, jnp.float32)
    if cuts:
        values = values * level_of(rng, extent, cuts, -0.22, 0.18)
    return jnp.clip(values, -bound, bound).astype(kind)


def setup_inputs(seed: int = 0) -> dict:
    key_list = jax.random.split(jax.random.key(seed), 9)
    return {
        "tokens": scatter_about(key_list[0], (TOKENS, D), 1.0, 6.0, ((0, 64), (1, 8))),
        "cotangent": scatter_about(key_list[1], (TOKENS, D), 1.0, 6.0, ((0, 64), (1, 8))),
        "gate_inner": scatter_about(key_list[2], (NB, BS, BS), BS ** -0.5, 0.5, ((0, 8), (1, 64))),
        "gate_outer": scatter_about(key_list[3], (NB, BS, BS), BS ** -0.5, 0.5, ((0, 8), (1, 64))),
        "value_inner": scatter_about(key_list[4], (NB, BS, BS), BS ** -0.5, 0.5, ((0, 8), (1, 64))),
        "value_outer": scatter_about(key_list[5], (NB, BS, BS), BS ** -0.5, 0.5, ((0, 8), (1, 64))),
        "down_inner": scatter_about(key_list[6], (NB, BS, BS), BS ** -0.5, 0.5, ((0, 8), (1, 64))),
        "down_outer": scatter_about(key_list[7], (NB, BS, BS), BS ** -0.5, 0.5, ((0, 8), (1, 64))),
    }


def blockwise(weights, values):
    return jnp.einsum('tbi,bio->tbo', values.astype(jnp.float32), weights.astype(jnp.float32))


def blockwise_back(weights, values):
    return jnp.einsum('tbo,bio->tbi', values.astype(jnp.float32), weights.astype(jnp.float32))


def block_outer(left, right):
    return jnp.einsum('tbi,tbo->bio', left.astype(jnp.float32), right.astype(jnp.float32))


def permute(values):
    count_tok, count_blocks, width = values.shape
    fold = width // count_blocks
    shaped = values.reshape(count_tok, count_blocks, count_blocks, fold)
    return shaped.transpose(0, 2, 1, 3).reshape(count_tok, count_blocks, width)


def reference(tokens, cotangent, gate_inner, gate_outer, value_inner, value_outer, down_inner, down_outer):
    scale = float(TOKENS) ** -0.5

    def one_block(totals, index):
        start = (index * TOK_DEV).astype(jnp.int32)
        token_rows = lax.dynamic_slice_in_dim(tokens, start, TOK_DEV, 0).reshape(TOK_DEV, NB, BS)
        cot_rows = lax.dynamic_slice_in_dim(cotangent, start, TOK_DEV, 0).reshape(TOK_DEV, NB, BS)
        gate_first = blockwise(gate_inner, token_rows).astype(jnp.bfloat16)
        value_first = blockwise(value_inner, token_rows).astype(jnp.bfloat16)
        gate_mixed = permute(gate_first)
        value_mixed = permute(value_first)
        gate_pre = blockwise(gate_outer, gate_mixed)
        value_pre = blockwise(value_outer, value_mixed)
        hidden = (jax.nn.silu(gate_pre) * value_pre).astype(jnp.bfloat16)
        down_mixed = permute(blockwise(down_inner, hidden).astype(jnp.bfloat16))
        mixed_rows = blockwise(down_outer, down_mixed).astype(jnp.bfloat16)
        grad_down_outer = block_outer(down_mixed, cot_rows)
        down_back = permute(blockwise_back(down_outer, cot_rows).astype(jnp.bfloat16))
        grad_down_inner = block_outer(hidden, down_back)
        hidden_back = blockwise_back(down_inner, down_back)
        sigma = jax.nn.sigmoid(gate_pre)
        gate_back = (hidden_back * value_pre * sigma * (1.0 + gate_pre * (1.0 - sigma))).astype(jnp.bfloat16)
        value_back = (hidden_back * gate_pre * sigma).astype(jnp.bfloat16)
        grad_gate_outer = block_outer(gate_mixed, gate_back)
        grad_value_outer = block_outer(value_mixed, value_back)
        gate_return = permute(blockwise_back(gate_outer, gate_back).astype(jnp.bfloat16))
        value_return = permute(blockwise_back(value_outer, value_back).astype(jnp.bfloat16))
        grad_gate_inner = block_outer(token_rows, gate_return)
        grad_value_inner = block_outer(token_rows, value_return)
        back_rows = (blockwise_back(gate_inner, gate_return) + blockwise_back(value_inner, value_return)).astype(jnp.bfloat16)
        fresh = (grad_gate_inner, grad_gate_outer, grad_value_inner, grad_value_outer, grad_down_inner, grad_down_outer)
        totals = tuple(total + term for total, term in zip(totals, fresh))
        return totals, (mixed_rows.reshape(TOK_DEV, D), back_rows.reshape(TOK_DEV, D))

    zeros = tuple(jnp.zeros((NB, BS, BS), jnp.float32) for _ in range(6))
    totals, (mixed_all, back_all) = lax.scan(one_block, zeros, jnp.arange(N_DP, dtype=jnp.int32))
    grads = tuple(total * scale for total in totals)
    return (mixed_all.reshape(TOKENS, D), back_all.reshape(TOKENS, D), grads[0], grads[1], grads[2], grads[3], grads[4], grads[5])
```

```python
import functools

import jax
import jax.numpy as jnp
from jax import lax
from jax.experimental import pallas as pl
from jax.experimental.pallas import tpu as pltpu
from jax.sharding import Mesh, PartitionSpec as P

BF = jnp.bfloat16
F32 = jnp.float32
AXES = ("xlo", "z", "core", "xhi", "y")
QUAD = ("xlo", "core")
PLANE = ("xhi", "y", "xlo", "core")
DP = ("xlo", "z", "core")
WIDTH = 128
PAIR = 256
TOK = 256
SLAB = 1024


def dot(left, right, left_dim, right_dim):
    return lax.dot_general(
        left, right, (((left_dim,), (right_dim,)), ((), ())), preferred_element_type=F32
    )


def one_hot(shape, test):
    rows = lax.broadcasted_iota(jnp.int32, shape, 0)
    cols = lax.broadcasted_iota(jnp.int32, shape, 1)
    return jnp.where(test(rows, cols), 1.0, 0.0).astype(BF)


def pairs_from_natural():
    return one_hot(
        (PAIR, PAIR),
        lambda r, c: c == ((r >> 1) & 1) * WIDTH + (r >> 2) * 2 + (r & 1),
    )


def natural_from_pairs():
    return one_hot(
        (PAIR, PAIR),
        lambda r, c: r == ((c >> 1) & 1) * WIDTH + (c >> 2) * 2 + (c & 1),
    )


def quads_from_natural():
    return one_hot(
        (PAIR, PAIR),
        lambda r, c: c == ((r >> 2) & 1) * WIDTH + (r >> 3) * 4 + (r & 3),
    )


def gathered_to_pairs(count_z):
    def test(r, c):
        inner = r & 7
        zed = (r >> 3) & (count_z - 1)
        xlo = (r >> 3) // count_z
        return c == (zed * 2 + xlo) * 8 + inner

    return one_hot((PAIR, PAIR), test)


def expand(factor):
    rows = lax.broadcasted_iota(jnp.int32, factor.shape, 0)
    first = ((rows >> 1) & 1) == 0
    zero = jnp.zeros_like(factor)
    return jnp.concatenate(
        [jnp.where(first, factor, zero), jnp.where(first, zero, factor)], axis=1
    )


def own_block(full):
    rows = lax.broadcasted_iota(jnp.int32, (PAIR, WIDTH), 0)
    return jnp.where(((rows >> 1) & 1) == 0, full[:, :WIDTH], full[:, WIDTH:])


def factor_of(rows, index):
    return expand(rows[:, index * WIDTH : (index + 1) * WIDTH])


def split_kernel(tok_ref, cot_ref, out_ref):
    for part in range(4):
        cols = slice(part * PAIR, (part + 1) * PAIR)
        out_ref[2 * part * TOK : (2 * part + 1) * TOK, :] = tok_ref[:, cols]
        out_ref[(2 * part + 1) * TOK : (2 * part + 2) * TOK, :] = cot_ref[:, cols]


def first_kernel(count_z, weights_ref, rows_ref, send_ref, weights_out_ref):
    weights = dot(gathered_to_pairs(count_z), weights_ref[...], 1, 0).astype(BF)
    weights_out_ref[...] = weights
    nat = natural_from_pairs()
    quads = quads_from_natural()
    gate = dot(quads, dot(nat, factor_of(weights, 0), 1, 0).astype(BF), 1, 1).astype(BF)
    value = dot(quads, dot(nat, factor_of(weights, 2), 1, 0).astype(BF), 1, 1).astype(BF)
    down = factor_of(weights, 5)
    for part in range(4):
        tok = rows_ref[2 * part * TOK : (2 * part + 1) * TOK, :]
        cot = rows_ref[(2 * part + 1) * TOK : (2 * part + 2) * TOK, :]
        at = part * TOK
        send_ref[:, at : at + TOK] = dot(gate, tok, 1, 1).astype(BF)
        send_ref[:, SLAB + at : SLAB + at + TOK] = dot(value, tok, 1, 1).astype(BF)
        send_ref[:, 2 * SLAB + at : 2 * SLAB + at + TOK] = dot(down, cot, 1, 1).astype(BF)


def middle_kernel(weights_ref, recv_ref, send_ref, grad_ref, hid_ref, gate_ref, value_ref):
    pairs = pairs_from_natural()
    quads = quads_from_natural()
    weights = weights_ref[...]
    gate_w = factor_of(weights, 1)
    value_w = factor_of(weights, 3)
    down_w = factor_of(weights, 4)
    gate_fwd = dot(pairs, gate_w, 1, 1).astype(BF)
    value_fwd = dot(pairs, value_w, 1, 1).astype(BF)
    gate_bwd = dot(gate_w, pairs, 1, 1).astype(BF)
    value_bwd = dot(value_w, pairs, 1, 1).astype(BF)
    down_fwd = dot(quads, down_w, 1, 1).astype(BF)
    down_bwd = dot(down_w, quads, 1, 1).astype(BF)
    for part in range(4):
        at = part * TOK
        cols = slice(at, at + TOK)
        gate_pre = dot(gate_fwd, recv_ref[:, cols], 1, 0)
        value_pre = dot(value_fwd, recv_ref[:, SLAB + at : SLAB + at + TOK], 1, 0)
        sigma = jax.nn.sigmoid(gate_pre)
        hidden = (gate_pre * sigma * value_pre).astype(BF)
        hid_ref[:, cols] = hidden
        send_ref[:, cols] = dot(down_fwd, hidden, 1, 0).astype(BF)
        back = dot(down_bwd, recv_ref[:, 2 * SLAB + at : 2 * SLAB + at + TOK], 1, 0)
        gate_back = (back * value_pre * sigma * (1.0 + gate_pre * (1.0 - sigma))).astype(BF)
        value_back = (back * gate_pre * sigma).astype(BF)
        gate_ref[:, cols] = gate_back
        value_ref[:, cols] = value_back
        send_ref[:, SLAB + at : SLAB + at + TOK] = dot(gate_bwd, gate_back, 1, 0).astype(BF)
        send_ref[:, 2 * SLAB + at : 2 * SLAB + at + TOK] = dot(
            value_bwd, value_back, 1, 0
        ).astype(BF)
    gate_grad = dot(recv_ref[:, :SLAB], gate_ref[...], 1, 1).astype(BF)
    value_grad = dot(recv_ref[:, SLAB : 2 * SLAB], value_ref[...], 1, 1).astype(BF)
    down_grad = dot(hid_ref[...], recv_ref[:, 2 * SLAB :], 1, 1).astype(BF)
    grad_ref[:, :WIDTH] = own_block(dot(gate_grad, pairs, 1, 0)).astype(BF)
    grad_ref[:, WIDTH : 2 * WIDTH] = own_block(dot(value_grad, pairs, 1, 0)).astype(BF)
    grad_ref[:, 2 * WIDTH :] = own_block(dot(down_grad, quads, 1, 0)).astype(BF)


def last_kernel(
    weights_ref, rows_ref, recv_ref, outer_ref, out_ref, grad_ref, left_ref, cot_ref
):
    pairs = pairs_from_natural()
    nat = natural_from_pairs()
    quads = quads_from_natural()
    weights = weights_ref[...]
    down = factor_of(weights, 5)
    gate = dot(nat, dot(factor_of(weights, 0), quads, 1, 1).astype(BF), 1, 0).astype(BF)
    value = dot(nat, dot(factor_of(weights, 2), quads, 1, 1).astype(BF), 1, 0).astype(BF)
    for part in range(4):
        at = part * TOK
        tok = rows_ref[2 * part * TOK : (2 * part + 1) * TOK, :]
        cot_ref[at : at + TOK, :] = rows_ref[(2 * part + 1) * TOK : (2 * part + 2) * TOK, :]
        left_ref[:, at : at + TOK] = dot(pairs, tok, 1, 1).astype(BF)
        mixed = dot(recv_ref[:, at : at + TOK], down, 0, 0)
        out_ref[2 * part * TOK : (2 * part + 1) * TOK, :] = mixed.astype(BF)
        back = dot(gate, recv_ref[:, SLAB + at : SLAB + at + TOK], 1, 0) + dot(
            value, recv_ref[:, 2 * SLAB + at : 2 * SLAB + at + TOK], 1, 0
        )
        out_ref[(2 * part + 1) * TOK : (2 * part + 2) * TOK, :] = back.T.astype(BF)
    gate_grad = dot(left_ref[...], recv_ref[:, SLAB : 2 * SLAB], 1, 1).astype(BF)
    value_grad = dot(left_ref[...], recv_ref[:, 2 * SLAB :], 1, 1).astype(BF)
    down_grad = dot(recv_ref[:, :SLAB], cot_ref[...], 1, 0)
    inner = jnp.concatenate(
        [
            own_block(dot(gate_grad, quads, 1, 0)).astype(BF),
            own_block(dot(value_grad, quads, 1, 0)).astype(BF),
            own_block(down_grad).astype(BF),
        ],
        axis=1,
    )
    for half in range(2):
        take = lambda group: one_hot(
            (PAIR, PAIR),
            lambda r, c: (((r >> 2) & 1) == group)
            & (c == half * WIDTH + (r >> 3) * 4 + (r & 3)),
        )
        grad_ref[half * PAIR : (half + 1) * PAIR, :] = (
            dot(take(0), outer_ref[...], 1, 0) + dot(take(1), inner, 1, 0)
        ).astype(BF)


def end_kernel(count_z, scale, rows_ref, grads_ref, mixed_ref, back_ref, *grad_refs):
    def test(r, c):
        inner = c & 3
        group = (c >> 2) & 1
        core = (c >> 3) & 1
        xlo = (c >> 4) // count_z
        return r == group * 16 + xlo * 8 + core * 4 + inner

    total = dot(one_hot((32, 2 * PAIR), test), grads_ref[...], 1, 0) * scale
    for group in range(2):
        for third in range(3):
            for block in range(8):
                row = group * 16 + block * 2
                grad_refs[group * 3 + third][block] = total[
                    row : row + 2, third * WIDTH : (third + 1) * WIDTH
                ]
    for part in range(4):
        cols = slice(part * PAIR, (part + 1) * PAIR)
        mixed_ref[:, cols] = rows_ref[2 * part * TOK : (2 * part + 1) * TOK, :]
        back_ref[:, cols] = rows_ref[(2 * part + 1) * TOK : (2 * part + 2) * TOK, :]


def call(kernel, name, outs, scratch=()):
    return pl.pallas_call(
        kernel,
        out_shape=outs,
        scratch_shapes=list(scratch),
        compiler_params=pltpu.CompilerParams(vmem_limit_bytes=40 * 1024 * 1024),
        name=name,
    )


def shape(dims, kind=BF):
    return jax.ShapeDtypeStruct(dims, kind)


def local(
    tokens, cotangent, gate_inner, gate_outer, value_inner, value_outer, down_inner, down_outer
):
    count_z = lax.axis_size("z")
    scale = float(tokens.shape[0] * lax.axis_size(DP)) ** (-0.5)
    quad = lax.axis_index(QUAD)

    mine = jnp.concatenate(
        [gate_inner, gate_outer, value_inner, value_outer, down_inner, down_outer], axis=0
    )
    near = lax.all_gather(mine, QUAD, axis=0, tiled=True).reshape(4, 6, 8, 2, WIDTH)
    near = lax.dynamic_slice_in_dim(near, quad * 2, 2, 2)
    near = near.transpose(0, 2, 3, 1, 4).reshape(16, 6 * WIDTH)

    rows = call(split_kernel, "split", shape((8 * TOK, PAIR)))(tokens, cotangent)
    rows = lax.all_to_all(rows, QUAD, split_axis=0, concat_axis=0, tiled=True)
    gathered = lax.all_gather(near, "z", axis=0, tiled=True)

    send, weights = call(
        functools.partial(first_kernel, count_z),
        "first",
        (shape((PAIR, 3 * SLAB)), shape((PAIR, 6 * WIDTH))),
    )(gathered, rows)
    recv = lax.all_to_all(send, PLANE, split_axis=0, concat_axis=0, tiled=True)
    send, outer_grads = call(
        middle_kernel,
        "middle",
        (shape((PAIR, 3 * SLAB)), shape((PAIR, 3 * WIDTH))),
        [pltpu.VMEM((PAIR, SLAB), BF)] * 3,
    )(weights, recv)
    recv = lax.all_to_all(send, PLANE, split_axis=0, concat_axis=0, tiled=True)
    out_rows, grads = call(
        last_kernel,
        "last",
        (shape((8 * TOK, PAIR)), shape((2 * PAIR, 3 * WIDTH))),
        [pltpu.VMEM((PAIR, SLAB), BF), pltpu.VMEM((SLAB, PAIR), BF)],
    )(weights, rows, recv, outer_grads)
    out_rows = lax.all_to_all(out_rows, QUAD, split_axis=0, concat_axis=0, tiled=True)
    grads = lax.all_to_all(grads, DP, split_axis=0, concat_axis=0, tiled=True)
    mixed, back, g_gate_o, g_value_o, g_down_i, g_gate_i, g_value_i, g_down_o = call(
        functools.partial(end_kernel, count_z, scale),
        "end",
        (shape((TOK, 4 * PAIR)),) * 2 + (shape((8, 2, WIDTH), F32),) * 6,
    )(out_rows, grads)
    return mixed, back, g_gate_i, g_gate_o, g_value_i, g_value_o, g_down_i, g_down_o


def solution(mesh):
    fine = Mesh(mesh.devices.reshape(2, 16, 2, 2, 4), AXES)
    rows = P(DP, ("xhi", "y"))
    factor = P(("xhi", "y"), DP, None)
    return jax.shard_map(
        local,
        mesh=fine,
        in_specs=(rows,) * 2 + (factor,) * 6,
        out_specs=(rows,) * 2 + (factor,) * 6,
        check_vma=False,
    )
```

```python
import functools

import jax
import jax.numpy as jnp
from jax import lax
from jax.experimental import pallas as pl
from jax.experimental.pallas import tpu as pltpu
from jax.sharding import Mesh, PartitionSpec as P

BF = jnp.bfloat16
F32 = jnp.float32
AXES = ("xlo", "z", "core", "xhi", "y")
QUAD = ("xlo", "core")
PLANE = ("xhi", "y", "xlo", "core")
DP = ("xlo", "z", "core")
WIDTH = 128
PAIR = 256
TOK = 256
SLAB = 1024


def dot(left, right, left_dim, right_dim):
    return lax.dot_general(
        left, right, (((left_dim,), (right_dim,)), ((), ())), preferred_element_type=F32
    )


def one_hot(shape, test):
    rows = lax.broadcasted_iota(jnp.int32, shape, 0)
    cols = lax.broadcasted_iota(jnp.int32, shape, 1)
    return jnp.where(test(rows, cols), 1.0, 0.0).astype(BF)


def pairs_from_natural():
    return one_hot(
        (PAIR, PAIR),
        lambda r, c: c == ((r >> 1) & 1) * WIDTH + (r >> 2) * 2 + (r & 1),
    )


def natural_from_pairs():
    return one_hot(
        (PAIR, PAIR),
        lambda r, c: r == ((c >> 1) & 1) * WIDTH + (c >> 2) * 2 + (c & 1),
    )


def quads_from_natural():
    return one_hot(
        (PAIR, PAIR),
        lambda r, c: c == ((r >> 2) & 1) * WIDTH + (r >> 3) * 4 + (r & 3),
    )


def gathered_to_pairs(count_z):
    def test(r, c):
        inner = r & 7
        zed = (r >> 3) & (count_z - 1)
        xlo = (r >> 3) // count_z
        return c == (zed * 2 + xlo) * 8 + inner

    return one_hot((PAIR, PAIR), test)


def expand(factor):
    rows = lax.broadcasted_iota(jnp.int32, factor.shape, 0)
    first = ((rows >> 1) & 1) == 0
    zero = jnp.zeros_like(factor)
    return jnp.concatenate(
        [jnp.where(first, factor, zero), jnp.where(first, zero, factor)], axis=1
    )


def own_block(full):
    rows = lax.broadcasted_iota(jnp.int32, (PAIR, WIDTH), 0)
    return jnp.where(((rows >> 1) & 1) == 0, full[:, :WIDTH], full[:, WIDTH:])


def factor_of(rows, index):
    return expand(rows[:, index * WIDTH : (index + 1) * WIDTH])


def pack_kernel(*refs):
    sources, (rows_ref, stack_ref) = refs[:8], refs[8:]
    for at, ref in enumerate(sources[2:]):
        stack_ref[at * 8 : (at + 1) * 8] = ref[...]
    for part in range(4):
        cols = slice(part * PAIR, (part + 1) * PAIR)
        for which in range(2):
            at = (2 * part + which) * TOK
            rows_ref[at : at + TOK, :] = sources[which][:, cols]


def first_kernel(count_z, weights_ref, rows_ref, send_ref, weights_out_ref):
    weights = dot(gathered_to_pairs(count_z), weights_ref[...], 1, 0).astype(BF)
    weights_out_ref[...] = weights
    nat = natural_from_pairs()
    quads = quads_from_natural()
    gate = dot(quads, dot(nat, factor_of(weights, 0), 1, 0).astype(BF), 1, 1).astype(BF)
    value = dot(quads, dot(nat, factor_of(weights, 2), 1, 0).astype(BF), 1, 1).astype(BF)
    down = factor_of(weights, 5)
    for part in range(4):
        tok = rows_ref[2 * part * TOK : (2 * part + 1) * TOK, :]
        cot = rows_ref[(2 * part + 1) * TOK : (2 * part + 2) * TOK, :]
        at = part * TOK
        send_ref[:, at : at + TOK] = dot(gate, tok, 1, 1).astype(BF)
        send_ref[:, SLAB + at : SLAB + at + TOK] = dot(value, tok, 1, 1).astype(BF)
        send_ref[:, 2 * SLAB + at : 2 * SLAB + at + TOK] = dot(down, cot, 1, 1).astype(BF)


def middle_kernel(weights_ref, recv_ref, send_ref, grad_ref, hid_ref, gate_ref, value_ref):
    pairs = pairs_from_natural()
    quads = quads_from_natural()
    weights = weights_ref[...]
    gate_w = factor_of(weights, 1)
    value_w = factor_of(weights, 3)
    down_w = factor_of(weights, 4)
    gate_fwd = dot(pairs, gate_w, 1, 1).astype(BF)
    value_fwd = dot(pairs, value_w, 1, 1).astype(BF)
    gate_bwd = dot(gate_w, pairs, 1, 1).astype(BF)
    value_bwd = dot(value_w, pairs, 1, 1).astype(BF)
    down_fwd = dot(quads, down_w, 1, 1).astype(BF)
    down_bwd = dot(down_w, quads, 1, 1).astype(BF)
    for part in range(4):
        at = part * TOK
        cols = slice(at, at + TOK)
        gate_pre = dot(gate_fwd, recv_ref[:, cols], 1, 0)
        value_pre = dot(value_fwd, recv_ref[:, SLAB + at : SLAB + at + TOK], 1, 0)
        sigma = jax.nn.sigmoid(gate_pre)
        hidden = (gate_pre * sigma * value_pre).astype(BF)
        hid_ref[:, cols] = hidden
        send_ref[:, cols] = dot(down_fwd, hidden, 1, 0).astype(BF)
        back = dot(down_bwd, recv_ref[:, 2 * SLAB + at : 2 * SLAB + at + TOK], 1, 0)
        gate_back = (back * value_pre * sigma * (1.0 + gate_pre * (1.0 - sigma))).astype(BF)
        value_back = (back * gate_pre * sigma).astype(BF)
        gate_ref[:, cols] = gate_back
        value_ref[:, cols] = value_back
        send_ref[:, SLAB + at : SLAB + at + TOK] = dot(gate_bwd, gate_back, 1, 0).astype(BF)
        send_ref[:, 2 * SLAB + at : 2 * SLAB + at + TOK] = dot(
            value_bwd, value_back, 1, 0
        ).astype(BF)
    gate_grad = dot(recv_ref[:, :SLAB], gate_ref[...], 1, 1).astype(BF)
    value_grad = dot(recv_ref[:, SLAB : 2 * SLAB], value_ref[...], 1, 1).astype(BF)
    down_grad = dot(hid_ref[...], recv_ref[:, 2 * SLAB :], 1, 1).astype(BF)
    grad_ref[:, :WIDTH] = own_block(dot(gate_grad, pairs, 1, 0)).astype(BF)
    grad_ref[:, WIDTH : 2 * WIDTH] = own_block(dot(value_grad, pairs, 1, 0)).astype(BF)
    grad_ref[:, 2 * WIDTH :] = own_block(dot(down_grad, quads, 1, 0)).astype(BF)


def owner_rows(half, group):
    return one_hot(
        (PAIR, PAIR),
        lambda r, c: (((r >> 2) & 1) == group)
        & (c == half * WIDTH + (r >> 3) * 4 + (r & 3)),
    )


def inner_kernel(rows_ref, recv_ref, outer_ref, grad_ref, left_ref, cot_ref):
    quads = quads_from_natural()
    pairs = pairs_from_natural()
    for part in range(4):
        at = part * TOK
        tok = rows_ref[2 * part * TOK : (2 * part + 1) * TOK, :]
        left_ref[:, at : at + TOK] = dot(pairs, tok, 1, 1).astype(BF)
        cot_ref[at : at + TOK, :] = rows_ref[(2 * part + 1) * TOK : (2 * part + 2) * TOK, :]
    gate_grad = dot(left_ref[...], recv_ref[:, SLAB : 2 * SLAB], 1, 1).astype(BF)
    value_grad = dot(left_ref[...], recv_ref[:, 2 * SLAB :], 1, 1).astype(BF)
    down_grad = dot(recv_ref[:, :SLAB], cot_ref[...], 1, 0)
    inner = jnp.concatenate(
        [
            own_block(dot(gate_grad, quads, 1, 0)).astype(BF),
            own_block(dot(value_grad, quads, 1, 0)).astype(BF),
            own_block(down_grad).astype(BF),
        ],
        axis=1,
    )
    for half in range(2):
        grad_ref[half * PAIR : (half + 1) * PAIR, :] = (
            dot(owner_rows(half, 0), outer_ref[...], 1, 0) + dot(owner_rows(half, 1), inner, 1, 0)
        ).astype(BF)


def output_kernel(quad_ref, weights_ref, recv_ref, *out_refs):
    nat = natural_from_pairs()
    quads = quads_from_natural()
    weights = weights_ref[...]
    down = factor_of(weights, 5)
    gate = dot(nat, dot(factor_of(weights, 0), quads, 1, 1).astype(BF), 1, 0).astype(BF)
    value = dot(nat, dot(factor_of(weights, 2), quads, 1, 1).astype(BF), 1, 0).astype(BF)
    quad = quad_ref[0]
    for hop in range(4):
        at = pl.multiple_of((quad ^ hop) * TOK, TOK)
        mixed = dot(recv_ref[:, pl.ds(at, TOK)], down, 0, 0)
        out_refs[hop][:TOK, :] = mixed.astype(BF)
        back = dot(gate, recv_ref[:, pl.ds(SLAB + at, TOK)], 1, 0) + dot(
            value, recv_ref[:, pl.ds(2 * SLAB + at, TOK)], 1, 0
        )
        out_refs[hop][TOK:, :] = back.T.astype(BF)


def place_kernel(quad_ref, own_ref, one_ref, two_ref, three_ref, mixed_ref, back_ref):
    for hop, ref in enumerate((own_ref, one_ref, two_ref, three_ref)):
        at = pl.multiple_of((quad_ref[0] ^ hop) * PAIR, PAIR)
        mixed_ref[:, pl.ds(at, PAIR)] = ref[:TOK, :]
        back_ref[:, pl.ds(at, PAIR)] = ref[TOK:, :]


def end_kernel(count_z, scale, grads_ref, *grad_refs):
    def test(r, c):
        inner = c & 3
        group = (c >> 2) & 1
        core = (c >> 3) & 1
        xlo = (c >> 4) // count_z
        return r == group * 16 + xlo * 8 + core * 4 + inner

    total = dot(one_hot((32, 2 * PAIR), test), grads_ref[...], 1, 0) * scale
    for group in range(2):
        for third in range(3):
            for block in range(8):
                row = group * 16 + block * 2
                grad_refs[group * 3 + third][block] = total[
                    row : row + 2, third * WIDTH : (third + 1) * WIDTH
                ]


def call(kernel, name, outs, scratch=(), room=40, **specs):
    return pl.pallas_call(
        kernel,
        out_shape=outs,
        scratch_shapes=list(scratch),
        compiler_params=pltpu.CompilerParams(vmem_limit_bytes=room * 1024 * 1024),
        name=name,
        **specs,
    )


def scalar_first(arrays):
    vmem = pl.BlockSpec(memory_space=pltpu.VMEM)
    return [pl.BlockSpec(memory_space=pltpu.SMEM)] + [vmem] * arrays


def shape(dims, kind=BF):
    return jax.ShapeDtypeStruct(dims, kind)


def local(
    tokens, cotangent, gate_inner, gate_outer, value_inner, value_outer, down_inner, down_outer
):
    count_z = lax.axis_size("z")
    scale = float(tokens.shape[0] * lax.axis_size(DP)) ** (-0.5)
    quad = lax.axis_index(QUAD)

    rows, mine = call(
        pack_kernel,
        "pack",
        (shape((8 * TOK, PAIR)), shape((48, 2, WIDTH))),
        room=60,
    )(
        tokens,
        cotangent,
        gate_inner,
        gate_outer,
        value_inner,
        value_outer,
        down_inner,
        down_outer,
    )
    near = lax.all_gather(mine, QUAD, axis=0, tiled=True).reshape(4, 6, 8, 2, WIDTH)
    near = lax.dynamic_slice_in_dim(near, quad * 2, 2, 2)
    near = near.transpose(0, 2, 3, 1, 4).reshape(16, 6 * WIDTH)
    near, rows = lax.optimization_barrier((near, rows))
    rows = lax.all_to_all(rows, QUAD, split_axis=0, concat_axis=0, tiled=True)
    gathered = lax.all_gather(near, "z", axis=0, tiled=True)

    wide, slab = shape((PAIR, 3 * SLAB)), pltpu.VMEM((PAIR, SLAB), BF)
    send, weights = call(
        functools.partial(first_kernel, count_z), "first", (wide, shape((PAIR, 6 * WIDTH)))
    )(gathered, rows)
    recv = lax.all_to_all(send, PLANE, split_axis=0, concat_axis=0, tiled=True)
    send, outer = call(middle_kernel, "middle", (wide, shape((PAIR, 3 * WIDTH))), [slab] * 3)(
        weights, recv
    )
    recv = lax.all_to_all(send, PLANE, split_axis=0, concat_axis=0, tiled=True)
    grads = call(
        inner_kernel,
        "inner",
        shape((2 * PAIR, 3 * WIDTH)),
        [slab, pltpu.VMEM((SLAB, PAIR), BF)],
    )(rows, recv, outer)
    grads = lax.all_to_all(grads, DP, split_axis=0, concat_axis=0, tiled=True)
    quad = jnp.reshape(quad, (1,))
    own, *away = call(
        output_kernel, "output", (shape((2 * TOK, PAIR)),) * 4, in_specs=scalar_first(2)
    )(quad, weights, recv)
    away = [
        lax.ppermute(part, QUAD, [(at, at ^ hop) for at in range(4)])
        for hop, part in enumerate(away, 1)
    ]
    mixed, back = call(
        place_kernel, "place", (shape((TOK, 4 * PAIR)),) * 2, in_specs=scalar_first(4)
    )(quad, own, *away)
    g_gate_o, g_value_o, g_down_i, g_gate_i, g_value_i, g_down_o = call(
        functools.partial(end_kernel, count_z, scale), "end", (shape((8, 2, WIDTH), F32),) * 6
    )(grads)
    return mixed, back, g_gate_i, g_gate_o, g_value_i, g_value_o, g_down_i, g_down_o


def solution(mesh):
    fine = Mesh(mesh.devices.reshape(2, 16, 2, 2, 4), AXES)
    rows = P(DP, ("xhi", "y"))
    factor = P(("xhi", "y"), DP, None)
    return jax.shard_map(
        local,
        mesh=fine,
        in_specs=(rows,) * 2 + (factor,) * 6,
        out_specs=(rows,) * 2 + (factor,) * 6,
        check_vma=False,
    )
```

```python
import functools

import jax
import jax.numpy as jnp
from jax import lax
from jax.experimental import pallas as pl
from jax.experimental.pallas import tpu as pltpu
from jax.sharding import Mesh, PartitionSpec as P

BF = jnp.bfloat16
F32 = jnp.float32
AXES = ("xlo", "z", "core", "xhi", "y")
QUAD = ("xlo", "core")
PLANE = ("xhi", "y", "xlo", "core")
DP = ("xlo", "z", "core")
WIDTH = 128
PAIR = 256
TOK = 256
SLAB = 1024


def dot(left, right, left_dim, right_dim):
    return lax.dot_general(
        left, right, (((left_dim,), (right_dim,)), ((), ())), preferred_element_type=F32
    )


def one_hot(shape, test):
    rows = lax.broadcasted_iota(jnp.int32, shape, 0)
    cols = lax.broadcasted_iota(jnp.int32, shape, 1)
    return jnp.where(test(rows, cols), 1.0, 0.0).astype(BF)


def pairs_from_natural():
    return one_hot(
        (PAIR, PAIR),
        lambda r, c: c == ((r >> 1) & 1) * WIDTH + (r >> 2) * 2 + (r & 1),
    )


def natural_from_pairs():
    return one_hot(
        (PAIR, PAIR),
        lambda r, c: r == ((c >> 1) & 1) * WIDTH + (c >> 2) * 2 + (c & 1),
    )


def quads_from_natural():
    return one_hot(
        (PAIR, PAIR),
        lambda r, c: c == ((r >> 2) & 1) * WIDTH + (r >> 3) * 4 + (r & 3),
    )


def group_rows(group):
    return one_hot((PAIR, 2 * PAIR), lambda r, c: c == (r >> 2) * 8 + group * 4 + (r & 3))


def owner_rows(group):
    return one_hot(
        (2 * PAIR, PAIR),
        lambda r, c: (((r >> 2) & 1) == group) & (c == (r >> 3) * 4 + (r & 3)),
    )


def expand(factor):
    rows = lax.broadcasted_iota(jnp.int32, factor.shape, 0)
    first = ((rows >> 1) & 1) == 0
    zero = jnp.zeros_like(factor)
    return jnp.concatenate(
        [jnp.where(first, factor, zero), jnp.where(first, zero, factor)], axis=1
    )


def own_block(full):
    rows = lax.broadcasted_iota(jnp.int32, (PAIR, WIDTH), 0)
    return jnp.where(((rows >> 1) & 1) == 0, full[:, :WIDTH], full[:, WIDTH:])


def factor_of(rows, index):
    return expand(rows[:, index * WIDTH : (index + 1) * WIDTH])


def share_kernel(count_z, *refs):
    factor_refs, (share_ref, rows_ref, sems) = refs[:6], refs[6:]
    copies = [
        pltpu.make_async_copy(ref, rows_ref.at[at], sems.at[at])
        for at, ref in enumerate(factor_refs)
    ]
    for copy in copies:
        copy.start()
    for copy in copies:
        copy.wait()
    for xlo in range(2):
        thirds = []
        for third in range(3):
            rows = [
                rows_ref[group * 3 + third, (xlo * 2 + core) * 2 + k].astype(F32)
                for core in range(2)
                for group in range(2)
                for k in range(2)
            ]
            thirds.append(jnp.concatenate(rows, axis=0).astype(BF))
        slab = jnp.concatenate(thirds, axis=1)
        for zed in range(count_z):
            at = (xlo * count_z + zed) * 16
            share_ref[at : at + 16, :] = slab


def cut_piece(quad_ref, tok_ref, cot_ref, hop, ref):
    cols = pl.ds(pl.multiple_of((quad_ref[0] ^ hop) * PAIR, PAIR), PAIR)
    ref[:TOK, :] = tok_ref[:, cols]
    ref[TOK:, :] = cot_ref[:, cols]


def far_kernel(quad_ref, tok_ref, cot_ref, two_ref, three_ref):
    cut_piece(quad_ref, tok_ref, cot_ref, 2, two_ref)
    cut_piece(quad_ref, tok_ref, cot_ref, 3, three_ref)


def near_kernel(quad_ref, tok_ref, cot_ref, after_ref, own_ref, one_ref, *order_refs):
    del after_ref
    cut_piece(quad_ref, tok_ref, cot_ref, 0, own_ref)
    cut_piece(quad_ref, tok_ref, cot_ref, 1, one_ref)
    pairs_ref, quads_ref, first_ref, second_ref = order_refs
    pairs_ref[...] = pairs_from_natural()
    quads_ref[...] = quads_from_natural()
    first_ref[...] = owner_rows(0)
    second_ref[...] = owner_rows(1)


def first_kernel(quad_ref, share_ref, *refs):
    piece_refs, (quads_ref, send_ref, weights_ref) = refs[:4], refs[4:]
    share, nat, quads = share_ref[...], natural_from_pairs(), quads_ref[...]
    weights = jnp.concatenate(
        [dot(group_rows(0), share, 1, 0), dot(group_rows(1), share, 1, 0)], axis=1
    ).astype(BF)
    weights_ref[...] = weights
    gate = dot(quads, dot(nat, factor_of(weights, 0), 1, 0).astype(BF), 1, 1).astype(BF)
    value = dot(quads, dot(nat, factor_of(weights, 1), 1, 0).astype(BF), 1, 1).astype(BF)
    down = factor_of(weights, 2)
    for hop, ref in enumerate(piece_refs):
        at = pl.multiple_of((quad_ref[0] ^ hop) * TOK, TOK)
        tok, cot = ref[:TOK, :], ref[TOK:, :]
        send_ref[:, pl.ds(at, TOK)] = dot(gate, tok, 1, 1).astype(BF)
        send_ref[:, pl.ds(SLAB + at, TOK)] = dot(value, tok, 1, 1).astype(BF)
        send_ref[:, pl.ds(2 * SLAB + at, TOK)] = dot(down, cot, 1, 1).astype(BF)


def middle_kernel(
    weights_ref,
    recv_ref,
    pairs_ref,
    quads_ref,
    send_ref,
    grad_ref,
    hid_ref,
    gate_ref,
    value_ref,
):
    pairs, quads = pairs_ref[...], quads_ref[...]
    weights = weights_ref[...]
    gate_w = factor_of(weights, 3)
    value_w = factor_of(weights, 4)
    down_w = factor_of(weights, 5)
    gate_fwd = dot(pairs, gate_w, 1, 1).astype(BF)
    value_fwd = dot(pairs, value_w, 1, 1).astype(BF)
    gate_bwd = dot(gate_w, pairs, 1, 1).astype(BF)
    value_bwd = dot(value_w, pairs, 1, 1).astype(BF)
    down_fwd = dot(quads, down_w, 1, 1).astype(BF)
    down_bwd = dot(down_w, quads, 1, 1).astype(BF)
    gate_pre = dot(gate_fwd, recv_ref[:, :SLAB], 1, 0)
    value_pre = dot(value_fwd, recv_ref[:, SLAB : 2 * SLAB], 1, 0)
    sigma = jax.nn.sigmoid(gate_pre)
    hidden = (gate_pre * sigma * value_pre).astype(BF)
    hid_ref[...] = hidden
    send_ref[:, :SLAB] = dot(down_fwd, hidden, 1, 0).astype(BF)
    back = dot(down_bwd, recv_ref[:, 2 * SLAB :], 1, 0)
    gate_back = (back * value_pre * sigma * (1.0 + gate_pre * (1.0 - sigma))).astype(BF)
    value_back = (back * gate_pre * sigma).astype(BF)
    gate_ref[...] = gate_back
    value_ref[...] = value_back
    send_ref[:, SLAB : 2 * SLAB] = dot(gate_bwd, gate_back, 1, 0).astype(BF)
    send_ref[:, 2 * SLAB :] = dot(value_bwd, value_back, 1, 0).astype(BF)
    gate_grad = dot(recv_ref[:, :SLAB], gate_ref[...], 1, 1).astype(BF)
    value_grad = dot(recv_ref[:, SLAB : 2 * SLAB], value_ref[...], 1, 1).astype(BF)
    down_grad = dot(hid_ref[...], recv_ref[:, 2 * SLAB :], 1, 1).astype(BF)
    grad_ref[:, :WIDTH] = own_block(dot(gate_grad, pairs, 1, 0)).astype(BF)
    grad_ref[:, WIDTH : 2 * WIDTH] = own_block(dot(value_grad, pairs, 1, 0)).astype(BF)
    grad_ref[:, 2 * WIDTH :] = own_block(dot(down_grad, quads, 1, 0)).astype(BF)


def inner_kernel(quad_ref, *refs):
    piece_refs, (recv_ref, outer_ref, pairs_ref, quads_ref, first_ref, second_ref, grad_ref) = (
        refs[:4],
        refs[4:],
    )
    pairs, quads = pairs_ref[...], quads_ref[...]
    gate_grad = value_grad = down_grad = 0.0
    for hop, ref in enumerate(piece_refs):
        at = pl.multiple_of((quad_ref[0] ^ hop) * TOK, TOK)
        tok, cot = ref[:TOK, :], ref[TOK:, :]
        gate_grad += dot(recv_ref[:, pl.ds(SLAB + at, TOK)], tok, 1, 0)
        value_grad += dot(recv_ref[:, pl.ds(2 * SLAB + at, TOK)], tok, 1, 0)
        down_grad += dot(recv_ref[:, pl.ds(at, TOK)], cot, 1, 0)
    gate_grad = dot(pairs, gate_grad.astype(BF), 1, 1).astype(BF)
    value_grad = dot(pairs, value_grad.astype(BF), 1, 1).astype(BF)
    inner = jnp.concatenate(
        [
            own_block(dot(gate_grad, quads, 1, 0)).astype(BF),
            own_block(dot(value_grad, quads, 1, 0)).astype(BF),
            own_block(down_grad).astype(BF),
        ],
        axis=1,
    )
    grad_ref[...] = (
        dot(first_ref[...], outer_ref[...], 1, 0) + dot(second_ref[...], inner, 1, 0)
    ).astype(BF)


def output_kernel(hops, quad_ref, weights_ref, recv_ref, *refs):
    out_refs = refs[-2:]
    nat = natural_from_pairs()
    quads = quads_from_natural()
    weights = weights_ref[...]
    down = factor_of(weights, 2)
    gate = dot(nat, dot(factor_of(weights, 0), quads, 1, 1).astype(BF), 1, 0).astype(BF)
    value = dot(nat, dot(factor_of(weights, 1), quads, 1, 1).astype(BF), 1, 0).astype(BF)
    quad = quad_ref[0]
    for hop, out_ref in zip(hops, out_refs):
        at = pl.multiple_of((quad ^ hop) * TOK, TOK)
        mixed = dot(recv_ref[:, pl.ds(at, TOK)], down, 0, 0)
        out_ref[:TOK, :] = mixed.astype(BF)
        back = dot(gate, recv_ref[:, pl.ds(SLAB + at, TOK)], 1, 0) + dot(
            value, recv_ref[:, pl.ds(2 * SLAB + at, TOK)], 1, 0
        )
        out_ref[TOK:, :] = back.T.astype(BF)


def place_kernel(quad_ref, own_ref, one_ref, two_ref, three_ref, mixed_ref, back_ref):
    for hop, ref in enumerate((own_ref, one_ref, two_ref, three_ref)):
        at = pl.multiple_of((quad_ref[0] ^ hop) * PAIR, PAIR)
        mixed_ref[:, pl.ds(at, PAIR)] = ref[:TOK, :]
        back_ref[:, pl.ds(at, PAIR)] = ref[TOK:, :]


def end_kernel(count_z, scale, grads_ref, *grad_refs):
    def test(r, c):
        inner = c & 3
        group = (c >> 2) & 1
        core = (c >> 3) & 1
        xlo = (c >> 4) // count_z
        return r == group * 16 + xlo * 8 + core * 4 + inner

    total = dot(one_hot((32, 2 * PAIR), test), grads_ref[...], 1, 0) * scale
    for group in range(2):
        for third in range(3):
            for block in range(8):
                row = group * 16 + block * 2
                grad_refs[group * 3 + third][block] = total[
                    row : row + 2, third * WIDTH : (third + 1) * WIDTH
                ]


def call(kernel, name, outs, scratch=(), room=40, **specs):
    return pl.pallas_call(
        kernel,
        out_shape=outs,
        scratch_shapes=list(scratch),
        compiler_params=pltpu.CompilerParams(vmem_limit_bytes=room * 1024 * 1024),
        name=name,
        **specs,
    )


def scalar_first(arrays):
    vmem = pl.BlockSpec(memory_space=pltpu.VMEM)
    return [pl.BlockSpec(memory_space=pltpu.SMEM)] + [vmem] * arrays


def swap(part, hop):
    return lax.ppermute(part, QUAD, [(at, at ^ hop) for at in range(4)])


def shape(dims, kind=BF):
    return jax.ShapeDtypeStruct(dims, kind)


def local(
    tokens, cotangent, gate_inner, gate_outer, value_inner, value_outer, down_inner, down_outer
):
    count_z = lax.axis_size("z")
    scale = float(tokens.shape[0] * lax.axis_size(DP)) ** (-0.5)

    quad = jnp.reshape(lax.axis_index(QUAD), (1,))
    piece, share = shape((2 * TOK, PAIR)), shape((2 * PAIR, 3 * WIDTH))
    shares = call(
        functools.partial(share_kernel, count_z),
        "share",
        share,
        [pltpu.VMEM((6, 8, 2, WIDTH), BF), pltpu.SemaphoreType.DMA((6,))],
        room=60,
        in_specs=[pl.BlockSpec(memory_space=pl.ANY)] * 6,
    )(gate_inner, value_inner, down_outer, gate_outer, value_outer, down_inner)
    shares = lax.all_to_all(shares, DP, split_axis=0, concat_axis=0, tiled=True)
    two, three = call(far_kernel, "far", (piece,) * 2, room=60, in_specs=scalar_first(2))(
        quad, tokens, cotangent
    )
    square, tall = shape((PAIR, PAIR)), shape((2 * PAIR, PAIR))
    after = [pl.BlockSpec(memory_space=pl.ANY)]
    own, one, pairs, quads, *owners = call(
        near_kernel,
        "near",
        (piece, piece, square, square, tall, tall),
        in_specs=scalar_first(2) + after,
    )(quad, tokens, cotangent, two)
    pieces = (own, swap(one, 1), swap(two, 2), swap(three, 3))

    wide, slab = shape((PAIR, 3 * SLAB)), pltpu.VMEM((PAIR, SLAB), BF)
    send, weights = call(
        first_kernel, "first", (wide, shape((PAIR, 6 * WIDTH))), in_specs=scalar_first(6)
    )(quad, shares, *pieces, quads)
    recv = lax.all_to_all(send, PLANE, split_axis=0, concat_axis=0, tiled=True)
    send, outer = call(middle_kernel, "middle", (wide, shape((PAIR, 3 * WIDTH))), [slab] * 3)(
        weights, recv, pairs, quads
    )
    recv = lax.all_to_all(send, PLANE, split_axis=0, concat_axis=0, tiled=True)
    grads = call(inner_kernel, "inner", share, in_specs=scalar_first(10))(
        quad, *pieces, recv, outer, pairs, quads, *owners
    )
    grads = lax.all_to_all(grads, DP, split_axis=0, concat_axis=0, tiled=True)
    two, three = call(
        functools.partial(output_kernel, (2, 3)), "output", (piece,) * 2, in_specs=scalar_first(2)
    )(quad, weights, recv)
    three = swap(three, 3)
    own, one = call(
        functools.partial(output_kernel, (0, 1)),
        "output2",
        (piece,) * 2,
        in_specs=scalar_first(2) + after,
    )(quad, weights, recv, three)
    mixed, back = call(
        place_kernel, "place", (shape((TOK, 4 * PAIR)),) * 2, in_specs=scalar_first(4)
    )(quad, own, swap(one, 1), swap(two, 2), three)
    g_gate_o, g_value_o, g_down_i, g_gate_i, g_value_i, g_down_o = call(
        functools.partial(end_kernel, count_z, scale), "end", (shape((8, 2, WIDTH), F32),) * 6
    )(grads)
    return mixed, back, g_gate_i, g_gate_o, g_value_i, g_value_o, g_down_i, g_down_o


def solution(mesh):
    fine = Mesh(mesh.devices.reshape(2, 16, 2, 2, 4), AXES)
    rows = P(DP, ("xhi", "y"))
    factor = P(("xhi", "y"), DP, None)
    return jax.shard_map(
        local,
        mesh=fine,
        in_specs=(rows,) * 2 + (factor,) * 6,
        out_specs=(rows,) * 2 + (factor,) * 6,
        check_vma=False,
    )
```

```python
import functools

import jax
import jax.numpy as jnp
from jax import lax
from jax.experimental import pallas as pl
from jax.experimental.pallas import tpu as pltpu
from jax.sharding import Mesh, PartitionSpec as P

BF = jnp.bfloat16
F32 = jnp.float32
AXES = ("xlo", "z", "core", "xhi", "y")
QUAD = ("xlo", "core")
PLANE = ("xhi", "y", "xlo", "core")
DP = ("xlo", "z", "core")
WIDTH = 128
PAIR = 256
TOK = 256
SLAB = 1024
STEP = 9


def dot(left, right, left_dim, right_dim):
    return lax.dot_general(
        left, right, (((left_dim,), (right_dim,)), ((), ())), preferred_element_type=F32
    )


def one_hot(shape, test):
    rows = lax.broadcasted_iota(jnp.int32, shape, 0)
    cols = lax.broadcasted_iota(jnp.int32, shape, 1)
    return jnp.where(test(rows, cols), 1.0, 0.0).astype(BF)


def pairs_from_natural():
    return one_hot(
        (PAIR, PAIR),
        lambda r, c: c == ((r >> 1) & 1) * WIDTH + (r >> 2) * 2 + (r & 1),
    )


def natural_from_pairs():
    return one_hot(
        (PAIR, PAIR),
        lambda r, c: r == ((c >> 1) & 1) * WIDTH + (c >> 2) * 2 + (c & 1),
    )


def quads_from_natural():
    return one_hot(
        (PAIR, PAIR),
        lambda r, c: c == ((r >> 2) & 1) * WIDTH + (r >> 3) * 4 + (r & 3),
    )


def device_at(place):
    return place >> 5, (((place >> 1) & 15) * STEP) & 15, place & 1


def place_of(device):
    return (device >> 5) * 32 + (((device >> 1) & 15) * STEP & 15) * 2 + (device & 1)


def device_index(place):
    xlo, zed, core = device_at(place)
    return xlo * 32 + zed * 2 + core


def group_rows(group):
    return one_hot(
        (PAIR, 2 * PAIR), lambda r, c: c == place_of(r >> 2) * 8 + group * 4 + (r & 3)
    )


def owner_rows(group):
    return one_hot(
        (2 * PAIR, PAIR),
        lambda r, c: (((r >> 2) & 1) == group) & (c == device_index(r >> 3) * 4 + (r & 3)),
    )


def expand(factor):
    rows = lax.broadcasted_iota(jnp.int32, factor.shape, 0)
    first = ((rows >> 1) & 1) == 0
    zero = jnp.zeros_like(factor)
    return jnp.concatenate(
        [jnp.where(first, factor, zero), jnp.where(first, zero, factor)], axis=1
    )


def own_block(full):
    rows = lax.broadcasted_iota(jnp.int32, (PAIR, WIDTH), 0)
    return jnp.where(((rows >> 1) & 1) == 0, full[:, :WIDTH], full[:, WIDTH:])


def factor_of(rows, index):
    return expand(rows[:, index * WIDTH : (index + 1) * WIDTH])


def share_kernel(*refs):
    factor_refs, (share_ref, rows_ref, sems) = refs[:6], refs[6:]
    copies = [
        pltpu.make_async_copy(ref, rows_ref.at[at], sems.at[at])
        for at, ref in enumerate(factor_refs)
    ]
    for copy in copies:
        copy.start()
    for copy in copies:
        copy.wait()
    slabs = {}
    for place in range(0, 64, 2):
        quads = tuple(device_at(at)[0] * 2 + device_at(at)[2] for at in (place, place + 1))
        if quads not in slabs:
            thirds = []
            for third in range(3):
                rows = [
                    rows_ref[group * 3 + third, quad * 2 + k].astype(F32)
                    for quad in quads
                    for group in range(2)
                    for k in range(2)
                ]
                thirds.append(jnp.concatenate(rows, axis=0).astype(BF))
            slabs[quads] = jnp.concatenate(thirds, axis=1)
        share_ref[place * 8 : place * 8 + 16, :] = slabs[quads]


def cut_piece(quad_ref, tok_ref, cot_ref, hop, ref):
    cols = pl.ds(pl.multiple_of((quad_ref[0] ^ hop) * PAIR, PAIR), PAIR)
    ref[:TOK, :] = tok_ref[:, cols]
    ref[TOK:, :] = cot_ref[:, cols]


def far_kernel(quad_ref, tok_ref, cot_ref, two_ref, three_ref):
    cut_piece(quad_ref, tok_ref, cot_ref, 2, two_ref)
    cut_piece(quad_ref, tok_ref, cot_ref, 3, three_ref)


def near_kernel(quad_ref, tok_ref, cot_ref, after_ref, own_ref, one_ref, *order_refs):
    del after_ref
    cut_piece(quad_ref, tok_ref, cot_ref, 0, own_ref)
    cut_piece(quad_ref, tok_ref, cot_ref, 1, one_ref)
    pairs_ref, quads_ref, first_ref, second_ref = order_refs
    pairs_ref[...] = pairs_from_natural()
    quads_ref[...] = quads_from_natural()
    first_ref[...] = owner_rows(0)
    second_ref[...] = owner_rows(1)


def first_kernel(quad_ref, share_ref, *refs):
    piece_refs, (quads_ref, send_ref, weights_ref) = refs[:4], refs[4:]
    share, nat, quads = share_ref[...], natural_from_pairs(), quads_ref[...]
    weights = jnp.concatenate(
        [dot(group_rows(0), share, 1, 0), dot(group_rows(1), share, 1, 0)], axis=1
    ).astype(BF)
    weights_ref[...] = weights
    gate = dot(quads, dot(nat, factor_of(weights, 0), 1, 0).astype(BF), 1, 1).astype(BF)
    value = dot(quads, dot(nat, factor_of(weights, 1), 1, 0).astype(BF), 1, 1).astype(BF)
    down = factor_of(weights, 2)
    for hop, ref in enumerate(piece_refs):
        at = pl.multiple_of((quad_ref[0] ^ hop) * TOK, TOK)
        tok, cot = ref[:TOK, :], ref[TOK:, :]
        send_ref[:, pl.ds(at, TOK)] = dot(gate, tok, 1, 1).astype(BF)
        send_ref[:, pl.ds(SLAB + at, TOK)] = dot(value, tok, 1, 1).astype(BF)
        send_ref[:, pl.ds(2 * SLAB + at, TOK)] = dot(down, cot, 1, 1).astype(BF)


def middle_kernel(
    weights_ref,
    recv_ref,
    pairs_ref,
    quads_ref,
    send_ref,
    grad_ref,
    hid_ref,
    gate_ref,
    value_ref,
):
    pairs, quads = pairs_ref[...], quads_ref[...]
    weights = weights_ref[...]
    gate_w = factor_of(weights, 3)
    value_w = factor_of(weights, 4)
    down_w = factor_of(weights, 5)
    gate_fwd = dot(pairs, gate_w, 1, 1).astype(BF)
    value_fwd = dot(pairs, value_w, 1, 1).astype(BF)
    gate_bwd = dot(gate_w, pairs, 1, 1).astype(BF)
    value_bwd = dot(value_w, pairs, 1, 1).astype(BF)
    down_fwd = dot(quads, down_w, 1, 1).astype(BF)
    down_bwd = dot(down_w, quads, 1, 1).astype(BF)
    gate_pre = dot(gate_fwd, recv_ref[:, :SLAB], 1, 0)
    value_pre = dot(value_fwd, recv_ref[:, SLAB : 2 * SLAB], 1, 0)
    sigma = jax.nn.sigmoid(gate_pre)
    hidden = (gate_pre * sigma * value_pre).astype(BF)
    hid_ref[...] = hidden
    send_ref[:, :SLAB] = dot(down_fwd, hidden, 1, 0).astype(BF)
    back = dot(down_bwd, recv_ref[:, 2 * SLAB :], 1, 0)
    gate_back = (back * value_pre * sigma * (1.0 + gate_pre * (1.0 - sigma))).astype(BF)
    value_back = (back * gate_pre * sigma).astype(BF)
    gate_ref[...] = gate_back
    value_ref[...] = value_back
    send_ref[:, SLAB : 2 * SLAB] = dot(gate_bwd, gate_back, 1, 0).astype(BF)
    send_ref[:, 2 * SLAB :] = dot(value_bwd, value_back, 1, 0).astype(BF)
    gate_grad = dot(recv_ref[:, :SLAB], gate_ref[...], 1, 1).astype(BF)
    value_grad = dot(recv_ref[:, SLAB : 2 * SLAB], value_ref[...], 1, 1).astype(BF)
    down_grad = dot(hid_ref[...], recv_ref[:, 2 * SLAB :], 1, 1).astype(BF)
    grad_ref[:, :WIDTH] = own_block(dot(gate_grad, pairs, 1, 0)).astype(BF)
    grad_ref[:, WIDTH : 2 * WIDTH] = own_block(dot(value_grad, pairs, 1, 0)).astype(BF)
    grad_ref[:, 2 * WIDTH :] = own_block(dot(down_grad, quads, 1, 0)).astype(BF)


def inner_kernel(quad_ref, *refs):
    piece_refs, (recv_ref, outer_ref, pairs_ref, quads_ref, first_ref, second_ref, grad_ref) = (
        refs[:4],
        refs[4:],
    )
    pairs, quads = pairs_ref[...], quads_ref[...]
    gate_grad = value_grad = down_grad = 0.0
    for hop, ref in enumerate(piece_refs):
        at = pl.multiple_of((quad_ref[0] ^ hop) * TOK, TOK)
        tok, cot = ref[:TOK, :], ref[TOK:, :]
        gate_grad += dot(recv_ref[:, pl.ds(SLAB + at, TOK)], tok, 1, 0)
        value_grad += dot(recv_ref[:, pl.ds(2 * SLAB + at, TOK)], tok, 1, 0)
        down_grad += dot(recv_ref[:, pl.ds(at, TOK)], cot, 1, 0)
    gate_grad = dot(pairs, gate_grad.astype(BF), 1, 1).astype(BF)
    value_grad = dot(pairs, value_grad.astype(BF), 1, 1).astype(BF)
    inner = jnp.concatenate(
        [
            own_block(dot(gate_grad, quads, 1, 0)).astype(BF),
            own_block(dot(value_grad, quads, 1, 0)).astype(BF),
            own_block(down_grad).astype(BF),
        ],
        axis=1,
    )
    grad_ref[...] = (
        dot(first_ref[...], outer_ref[...], 1, 0) + dot(second_ref[...], inner, 1, 0)
    ).astype(BF)


def output_kernel(hops, quad_ref, weights_ref, recv_ref, *refs):
    out_refs = refs[-2:]
    nat = natural_from_pairs()
    quads = quads_from_natural()
    weights = weights_ref[...]
    down = factor_of(weights, 2)
    gate = dot(nat, dot(factor_of(weights, 0), quads, 1, 1).astype(BF), 1, 0).astype(BF)
    value = dot(nat, dot(factor_of(weights, 1), quads, 1, 1).astype(BF), 1, 0).astype(BF)
    quad = quad_ref[0]
    for hop, out_ref in zip(hops, out_refs):
        at = pl.multiple_of((quad ^ hop) * TOK, TOK)
        mixed = dot(recv_ref[:, pl.ds(at, TOK)], down, 0, 0)
        out_ref[:TOK, :] = mixed.astype(BF)
        back = dot(gate, recv_ref[:, pl.ds(SLAB + at, TOK)], 1, 0) + dot(
            value, recv_ref[:, pl.ds(2 * SLAB + at, TOK)], 1, 0
        )
        out_ref[TOK:, :] = back.T.astype(BF)


def place_kernel(quad_ref, own_ref, one_ref, two_ref, three_ref, mixed_ref, back_ref):
    for hop, ref in enumerate((own_ref, one_ref, two_ref, three_ref)):
        at = pl.multiple_of((quad_ref[0] ^ hop) * PAIR, PAIR)
        mixed_ref[:, pl.ds(at, PAIR)] = ref[:TOK, :]
        back_ref[:, pl.ds(at, PAIR)] = ref[TOK:, :]


def end_kernel(scale, grads_ref, *grad_refs):
    def test(r, c):
        xlo, _, core = device_at(c >> 3)
        return r == ((c >> 2) & 1) * 16 + xlo * 8 + core * 4 + (c & 3)

    total = dot(one_hot((32, 2 * PAIR), test), grads_ref[...], 1, 0) * scale
    for group in range(2):
        for third in range(3):
            for block in range(8):
                row = group * 16 + block * 2
                grad_refs[group * 3 + third][block] = total[
                    row : row + 2, third * WIDTH : (third + 1) * WIDTH
                ]


def call(kernel, name, outs, scratch=(), room=40, **specs):
    return pl.pallas_call(
        kernel,
        out_shape=outs,
        scratch_shapes=list(scratch),
        compiler_params=pltpu.CompilerParams(vmem_limit_bytes=room * 1024 * 1024),
        name=name,
        **specs,
    )


def scalar_first(arrays):
    vmem = pl.BlockSpec(memory_space=pltpu.VMEM)
    return [pl.BlockSpec(memory_space=pltpu.SMEM)] + [vmem] * arrays


def exchange(rows):
    order = [[device_index(place) for place in range(64)]]
    return lax.all_to_all(
        rows, DP, split_axis=0, concat_axis=0, axis_index_groups=order, tiled=True
    )


def swap(part, hop):
    return lax.ppermute(part, QUAD, [(at, at ^ hop) for at in range(4)])


def shape(dims, kind=BF):
    return jax.ShapeDtypeStruct(dims, kind)


def local(
    tokens, cotangent, gate_inner, gate_outer, value_inner, value_outer, down_inner, down_outer
):
    scale = float(tokens.shape[0] * lax.axis_size(DP)) ** (-0.5)

    quad = jnp.reshape(lax.axis_index(QUAD), (1,))
    piece, share = shape((2 * TOK, PAIR)), shape((2 * PAIR, 3 * WIDTH))
    shares = call(
        share_kernel,
        "share",
        share,
        [pltpu.VMEM((6, 8, 2, WIDTH), BF), pltpu.SemaphoreType.DMA((6,))],
        room=60,
        in_specs=[pl.BlockSpec(memory_space=pl.ANY)] * 6,
    )(gate_inner, value_inner, down_outer, gate_outer, value_outer, down_inner)
    shares = exchange(shares)
    two, three = call(far_kernel, "far", (piece,) * 2, room=60, in_specs=scalar_first(2))(
        quad, tokens, cotangent
    )
    square, tall = shape((PAIR, PAIR)), shape((2 * PAIR, PAIR))
    after = [pl.BlockSpec(memory_space=pl.ANY)]
    own, one, pairs, quads, *owners = call(
        near_kernel,
        "near",
        (piece, piece, square, square, tall, tall),
        in_specs=scalar_first(2) + after,
    )(quad, tokens, cotangent, two)
    pieces = (own, swap(one, 1), swap(two, 2), swap(three, 3))

    wide, slab = shape((PAIR, 3 * SLAB)), pltpu.VMEM((PAIR, SLAB), BF)
    send, weights = call(
        first_kernel, "first", (wide, shape((PAIR, 6 * WIDTH))), in_specs=scalar_first(6)
    )(quad, shares, *pieces, quads)
    recv = lax.all_to_all(send, PLANE, split_axis=0, concat_axis=0, tiled=True)
    send, outer = call(middle_kernel, "middle", (wide, shape((PAIR, 3 * WIDTH))), [slab] * 3)(
        weights, recv, pairs, quads
    )
    recv = lax.all_to_all(send, PLANE, split_axis=0, concat_axis=0, tiled=True)
    grads = call(inner_kernel, "inner", share, in_specs=scalar_first(10))(
        quad, *pieces, recv, outer, pairs, quads, *owners
    )
    grads = exchange(grads)
    two, three = call(
        functools.partial(output_kernel, (2, 3)), "output", (piece,) * 2, in_specs=scalar_first(2)
    )(quad, weights, recv)
    three = swap(three, 3)
    own, one = call(
        functools.partial(output_kernel, (0, 1)),
        "output2",
        (piece,) * 2,
        in_specs=scalar_first(2) + after,
    )(quad, weights, recv, three)
    mixed, back = call(
        place_kernel, "place", (shape((TOK, 4 * PAIR)),) * 2, in_specs=scalar_first(4)
    )(quad, own, swap(one, 1), swap(two, 2), three)
    g_gate_o, g_value_o, g_down_i, g_gate_i, g_value_i, g_down_o = call(
        functools.partial(end_kernel, scale), "end", (shape((8, 2, WIDTH), F32),) * 6
    )(grads)
    return mixed, back, g_gate_i, g_gate_o, g_value_i, g_value_o, g_down_i, g_down_o


def solution(mesh):
    fine = Mesh(mesh.devices.reshape(2, 16, 2, 2, 4), AXES)
    rows = P(DP, ("xhi", "y"))
    factor = P(("xhi", "y"), DP, None)
    return jax.shard_map(
        local,
        mesh=fine,
        in_specs=(rows,) * 2 + (factor,) * 6,
        out_specs=(rows,) * 2 + (factor,) * 6,
        check_vma=False,
    )
```

```python
import functools

import jax
import jax.numpy as jnp
from jax import lax
from jax.experimental import pallas as pl
from jax.experimental.pallas import tpu as pltpu
from jax.sharding import Mesh, PartitionSpec as P

BF = jnp.bfloat16
F32 = jnp.float32
AXES = ("xlo", "z", "core", "xhi", "y")
QUAD = ("xlo", "core")
PLANE = ("xhi", "y", "xlo", "core")
DP = ("xlo", "z", "core")
WIDTH = 128
PAIR = 256
TOK = 256
SLAB = 1024
STEP = 9


def dot(left, right, left_dim, right_dim):
    return lax.dot_general(
        left, right, (((left_dim,), (right_dim,)), ((), ())), preferred_element_type=F32
    )


def one_hot(shape, test):
    rows = lax.broadcasted_iota(jnp.int32, shape, 0)
    cols = lax.broadcasted_iota(jnp.int32, shape, 1)
    return jnp.where(test(rows, cols), 1.0, 0.0).astype(BF)


def pairs_from_natural():
    return one_hot(
        (PAIR, PAIR),
        lambda r, c: c == ((r >> 1) & 1) * WIDTH + (r >> 2) * 2 + (r & 1),
    )


def natural_from_pairs():
    return one_hot(
        (PAIR, PAIR),
        lambda r, c: r == ((c >> 1) & 1) * WIDTH + (c >> 2) * 2 + (c & 1),
    )


def quads_from_natural():
    return one_hot(
        (PAIR, PAIR),
        lambda r, c: c == ((r >> 2) & 1) * WIDTH + (r >> 3) * 4 + (r & 3),
    )


def device_at(place):
    return place >> 5, (((place >> 1) & 15) * STEP) & 15, place & 1


def place_of(device):
    return (device >> 5) * 32 + (((device >> 1) & 15) * STEP & 15) * 2 + (device & 1)


def device_index(place):
    xlo, zed, core = device_at(place)
    return xlo * 32 + zed * 2 + core


def group_rows(group):
    return one_hot(
        (PAIR, 2 * PAIR), lambda r, c: c == place_of(r >> 2) * 8 + group * 4 + (r & 3)
    )


def owner_rows(group):
    return one_hot(
        (2 * PAIR, PAIR),
        lambda r, c: (((r >> 2) & 1) == group) & (c == device_index(r >> 3) * 4 + (r & 3)),
    )


def expand(factor):
    rows = lax.broadcasted_iota(jnp.int32, factor.shape, 0)
    first = ((rows >> 1) & 1) == 0
    zero = jnp.zeros_like(factor)
    return jnp.concatenate(
        [jnp.where(first, factor, zero), jnp.where(first, zero, factor)], axis=1
    )


def own_block(full):
    rows = lax.broadcasted_iota(jnp.int32, (PAIR, WIDTH), 0)
    return jnp.where(((rows >> 1) & 1) == 0, full[:, :WIDTH], full[:, WIDTH:])


def factor_of(rows, index):
    return expand(rows[:, index * WIDTH : (index + 1) * WIDTH])


def share_kernel(*refs):
    factor_refs, (share_ref, rows_ref, sems) = refs[:6], refs[6:]
    copies = [
        pltpu.make_async_copy(ref, rows_ref.at[at], sems.at[at])
        for at, ref in enumerate(factor_refs)
    ]
    for copy in copies:
        copy.start()
    for copy in copies:
        copy.wait()
    slabs = {}
    for place in range(0, 64, 2):
        quads = tuple(device_at(at)[0] * 2 + device_at(at)[2] for at in (place, place + 1))
        if quads not in slabs:
            thirds = []
            for third in range(3):
                rows = [
                    rows_ref[group * 3 + third, quad * 2 + k].astype(F32)
                    for quad in quads
                    for group in range(2)
                    for k in range(2)
                ]
                thirds.append(jnp.concatenate(rows, axis=0).astype(BF))
            slabs[quads] = jnp.concatenate(thirds, axis=1)
        share_ref[place * 8 : place * 8 + 16, :] = slabs[quads]


def cut_piece(quad_ref, tok_ref, cot_ref, hop, ref):
    cols = pl.ds(pl.multiple_of((quad_ref[0] ^ hop) * PAIR, PAIR), PAIR)
    ref[:TOK, :] = tok_ref[:, cols]
    ref[TOK:, :] = cot_ref[:, cols]


def far_kernel(quad_ref, tok_ref, cot_ref, two_ref, three_ref, sems):
    copies = []
    for at, ref in enumerate((two_ref, three_ref)):
        cols = pl.ds(pl.multiple_of((quad_ref[0] ^ (2 + at)) * PAIR, PAIR), PAIR)
        for which, source in enumerate((tok_ref, cot_ref)):
            copies.append(
                pltpu.make_async_copy(
                    source.at[:, cols],
                    ref.at[which * TOK : (which + 1) * TOK, :],
                    sems.at[2 * at + which],
                )
            )
    for copy in copies:
        copy.start()
    for copy in copies:
        copy.wait()


def near_kernel(quad_ref, tok_ref, cot_ref, after_ref, own_ref, one_ref, *order_refs):
    del after_ref
    cut_piece(quad_ref, tok_ref, cot_ref, 0, own_ref)
    cut_piece(quad_ref, tok_ref, cot_ref, 1, one_ref)
    pairs_ref, quads_ref, first_ref, second_ref = order_refs
    pairs_ref[...] = pairs_from_natural()
    quads_ref[...] = quads_from_natural()
    first_ref[...] = owner_rows(0)
    second_ref[...] = owner_rows(1)


def first_kernel(quad_ref, share_ref, *refs):
    piece_refs, (quads_ref, send_ref, weights_ref) = refs[:4], refs[4:]
    share, nat, quads = share_ref[...], natural_from_pairs(), quads_ref[...]
    weights = jnp.concatenate(
        [dot(group_rows(0), share, 1, 0), dot(group_rows(1), share, 1, 0)], axis=1
    ).astype(BF)
    weights_ref[...] = weights
    gate = dot(quads, dot(nat, factor_of(weights, 0), 1, 0).astype(BF), 1, 1).astype(BF)
    value = dot(quads, dot(nat, factor_of(weights, 1), 1, 0).astype(BF), 1, 1).astype(BF)
    down = factor_of(weights, 2)
    tok = jnp.concatenate([ref[:TOK, :] for ref in piece_refs], axis=0)
    cot = jnp.concatenate([ref[TOK:, :] for ref in piece_refs], axis=0)
    first = dot(jnp.concatenate([gate, value], axis=0), tok, 1, 1).astype(BF)
    back = dot(down, cot, 1, 1).astype(BF)
    for hop in range(4):
        at = pl.multiple_of((quad_ref[0] ^ hop) * TOK, TOK)
        cols = slice(hop * TOK, (hop + 1) * TOK)
        send_ref[:, pl.ds(at, TOK)] = first[:PAIR, cols]
        send_ref[:, pl.ds(SLAB + at, TOK)] = first[PAIR:, cols]
        send_ref[:, pl.ds(2 * SLAB + at, TOK)] = back[:, cols]


def middle_kernel(
    weights_ref,
    recv_ref,
    pairs_ref,
    quads_ref,
    send_ref,
    grad_ref,
    hid_ref,
    gate_ref,
    value_ref,
):
    pairs, quads = pairs_ref[...], quads_ref[...]
    weights = weights_ref[...]
    gate_w = factor_of(weights, 3)
    value_w = factor_of(weights, 4)
    down_w = factor_of(weights, 5)
    gate_fwd = dot(pairs, gate_w, 1, 1).astype(BF)
    value_fwd = dot(pairs, value_w, 1, 1).astype(BF)
    gate_bwd = dot(gate_w, pairs, 1, 1).astype(BF)
    value_bwd = dot(value_w, pairs, 1, 1).astype(BF)
    down_fwd = dot(quads, down_w, 1, 1).astype(BF)
    down_bwd = dot(down_w, quads, 1, 1).astype(BF)
    gate_pre = dot(gate_fwd, recv_ref[:, :SLAB], 1, 0)
    value_pre = dot(value_fwd, recv_ref[:, SLAB : 2 * SLAB], 1, 0)
    sigma = jax.nn.sigmoid(gate_pre)
    hidden = (gate_pre * sigma * value_pre).astype(BF)
    hid_ref[...] = hidden
    send_ref[:, :SLAB] = dot(down_fwd, hidden, 1, 0).astype(BF)
    back = dot(down_bwd, recv_ref[:, 2 * SLAB :], 1, 0)
    gate_back = (back * value_pre * sigma * (1.0 + gate_pre * (1.0 - sigma))).astype(BF)
    value_back = (back * gate_pre * sigma).astype(BF)
    gate_ref[...] = gate_back
    value_ref[...] = value_back
    send_ref[:, SLAB : 2 * SLAB] = dot(gate_bwd, gate_back, 1, 0).astype(BF)
    send_ref[:, 2 * SLAB :] = dot(value_bwd, value_back, 1, 0).astype(BF)
    gate_grad = dot(recv_ref[:, :SLAB], gate_ref[...], 1, 1).astype(BF)
    value_grad = dot(recv_ref[:, SLAB : 2 * SLAB], value_ref[...], 1, 1).astype(BF)
    down_grad = dot(hid_ref[...], recv_ref[:, 2 * SLAB :], 1, 1).astype(BF)
    grad_ref[:, :WIDTH] = own_block(dot(gate_grad, pairs, 1, 0)).astype(BF)
    grad_ref[:, WIDTH : 2 * WIDTH] = own_block(dot(value_grad, pairs, 1, 0)).astype(BF)
    grad_ref[:, 2 * WIDTH :] = own_block(dot(down_grad, quads, 1, 0)).astype(BF)


def inner_kernel(quad_ref, *refs):
    piece_refs, (recv_ref, outer_ref, pairs_ref, quads_ref, first_ref, second_ref, grad_ref) = (
        refs[:4],
        refs[4:],
    )
    pairs, quads = pairs_ref[...], quads_ref[...]
    tok = jnp.concatenate([ref[:TOK, :] for ref in piece_refs], axis=0)
    cot = jnp.concatenate([ref[TOK:, :] for ref in piece_refs], axis=0)

    def columns(first):
        at = [first + pl.multiple_of((quad_ref[0] ^ hop) * TOK, TOK) for hop in range(4)]
        return jnp.concatenate([recv_ref[:, pl.ds(start, TOK)] for start in at], axis=1)

    both = dot(jnp.concatenate([columns(SLAB), columns(2 * SLAB)], axis=0), tok, 1, 0)
    down_grad = dot(columns(0), cot, 1, 0)
    both = dot(pairs, both.astype(BF), 1, 1).astype(BF)
    gate_grad, value_grad = both[:, :PAIR], both[:, PAIR:]
    inner = jnp.concatenate(
        [
            own_block(dot(gate_grad, quads, 1, 0)).astype(BF),
            own_block(dot(value_grad, quads, 1, 0)).astype(BF),
            own_block(down_grad).astype(BF),
        ],
        axis=1,
    )
    grad_ref[...] = (
        dot(first_ref[...], outer_ref[...], 1, 0) + dot(second_ref[...], inner, 1, 0)
    ).astype(BF)


def output_kernel(hops, quad_ref, weights_ref, recv_ref, *refs):
    out_refs = refs[-2:]
    nat = natural_from_pairs()
    quads = quads_from_natural()
    weights = weights_ref[...]
    down = factor_of(weights, 2)
    gate = dot(nat, dot(factor_of(weights, 0), quads, 1, 1).astype(BF), 1, 0).astype(BF)
    value = dot(nat, dot(factor_of(weights, 1), quads, 1, 1).astype(BF), 1, 0).astype(BF)
    quad = quad_ref[0]
    for hop, out_ref in zip(hops, out_refs):
        at = pl.multiple_of((quad ^ hop) * TOK, TOK)
        mixed = dot(recv_ref[:, pl.ds(at, TOK)], down, 0, 0)
        out_ref[:TOK, :] = mixed.astype(BF)
        back = dot(gate, recv_ref[:, pl.ds(SLAB + at, TOK)], 1, 0) + dot(
            value, recv_ref[:, pl.ds(2 * SLAB + at, TOK)], 1, 0
        )
        out_ref[TOK:, :] = back.T.astype(BF)


def place_kernel(quad_ref, own_ref, one_ref, two_ref, three_ref, mixed_ref, back_ref):
    for hop, ref in enumerate((own_ref, one_ref, two_ref, three_ref)):
        at = pl.multiple_of((quad_ref[0] ^ hop) * PAIR, PAIR)
        mixed_ref[:, pl.ds(at, PAIR)] = ref[:TOK, :]
        back_ref[:, pl.ds(at, PAIR)] = ref[TOK:, :]


def end_kernel(scale, grads_ref, *grad_refs):
    def test(r, c):
        xlo, _, core = device_at(c >> 3)
        return r == ((c >> 2) & 1) * 16 + xlo * 8 + core * 4 + (c & 3)

    total = dot(one_hot((32, 2 * PAIR), test), grads_ref[...], 1, 0) * scale
    for group in range(2):
        for third in range(3):
            for block in range(8):
                row = group * 16 + block * 2
                grad_refs[group * 3 + third][block] = total[
                    row : row + 2, third * WIDTH : (third + 1) * WIDTH
                ]


def call(kernel, name, outs, scratch=(), room=40, **specs):
    return pl.pallas_call(
        kernel,
        out_shape=outs,
        scratch_shapes=list(scratch),
        compiler_params=pltpu.CompilerParams(vmem_limit_bytes=room * 1024 * 1024),
        name=name,
        **specs,
    )


def scalar_first(arrays):
    vmem = pl.BlockSpec(memory_space=pltpu.VMEM)
    return [pl.BlockSpec(memory_space=pltpu.SMEM)] + [vmem] * arrays


def exchange(rows):
    order = [[device_index(place) for place in range(64)]]
    return lax.all_to_all(
        rows, DP, split_axis=0, concat_axis=0, axis_index_groups=order, tiled=True
    )


def swap(part, hop):
    return lax.ppermute(part, QUAD, [(at, at ^ hop) for at in range(4)])


def shape(dims, kind=BF):
    return jax.ShapeDtypeStruct(dims, kind)


def local(
    tokens, cotangent, gate_inner, gate_outer, value_inner, value_outer, down_inner, down_outer
):
    scale = float(tokens.shape[0] * lax.axis_size(DP)) ** (-0.5)

    quad = jnp.reshape(lax.axis_index(QUAD), (1,))
    piece, share = shape((2 * TOK, PAIR)), shape((2 * PAIR, 3 * WIDTH))
    shares = call(
        share_kernel,
        "share",
        share,
        [pltpu.VMEM((6, 8, 2, WIDTH), BF), pltpu.SemaphoreType.DMA((6,))],
        room=60,
        in_specs=[pl.BlockSpec(memory_space=pl.ANY)] * 6,
    )(gate_inner, value_inner, down_outer, gate_outer, value_outer, down_inner)
    shares = exchange(shares)
    anywhere = pl.BlockSpec(memory_space=pl.ANY)
    two, three = call(
        far_kernel,
        "far",
        (piece,) * 2,
        [pltpu.SemaphoreType.DMA((4,))],
        room=60,
        in_specs=scalar_first(0) + [anywhere] * 2,
    )(quad, tokens, cotangent)
    square, tall = shape((PAIR, PAIR)), shape((2 * PAIR, PAIR))
    after = [anywhere]
    own, one, pairs, quads, *owners = call(
        near_kernel,
        "near",
        (piece, piece, square, square, tall, tall),
        in_specs=scalar_first(2) + after,
    )(quad, tokens, cotangent, two)
    pieces = (own, swap(one, 1), swap(two, 2), swap(three, 3))

    wide, slab = shape((PAIR, 3 * SLAB)), pltpu.VMEM((PAIR, SLAB), BF)
    send, weights = call(
        first_kernel, "first", (wide, shape((PAIR, 6 * WIDTH))), in_specs=scalar_first(6)
    )(quad, shares, *pieces, quads)
    recv = lax.all_to_all(send, PLANE, split_axis=0, concat_axis=0, tiled=True)
    send, outer = call(middle_kernel, "middle", (wide, shape((PAIR, 3 * WIDTH))), [slab] * 3)(
        weights, recv, pairs, quads
    )
    recv = lax.all_to_all(send, PLANE, split_axis=0, concat_axis=0, tiled=True)
    grads = call(inner_kernel, "inner", share, in_specs=scalar_first(10))(
        quad, *pieces, recv, outer, pairs, quads, *owners
    )
    grads = exchange(grads)
    two, three = call(
        functools.partial(output_kernel, (2, 3)), "output", (piece,) * 2, in_specs=scalar_first(2)
    )(quad, weights, recv)
    three = swap(three, 3)
    own, one = call(
        functools.partial(output_kernel, (0, 1)),
        "output2",
        (piece,) * 2,
        in_specs=scalar_first(2) + after,
    )(quad, weights, recv, three)
    mixed, back = call(
        place_kernel, "place", (shape((TOK, 4 * PAIR)),) * 2, in_specs=scalar_first(4)
    )(quad, own, swap(one, 1), swap(two, 2), three)
    g_gate_o, g_value_o, g_down_i, g_gate_i, g_value_i, g_down_o = call(
        functools.partial(end_kernel, scale), "end", (shape((8, 2, WIDTH), F32),) * 6
    )(grads)
    return mixed, back, g_gate_i, g_gate_o, g_value_i, g_value_o, g_down_i, g_down_o


def solution(mesh):
    fine = Mesh(mesh.devices.reshape(2, 16, 2, 2, 4), AXES)
    rows = P(DP, ("xhi", "y"))
    factor = P(("xhi", "y"), DP, None)
    return jax.shard_map(
        local,
        mesh=fine,
        in_specs=(rows,) * 2 + (factor,) * 6,
        out_specs=(rows,) * 2 + (factor,) * 6,
        check_vma=False,
    )
```

```python
import functools

import jax
import jax.numpy as jnp
from jax import lax
from jax.experimental import pallas as pl
from jax.experimental.pallas import tpu as pltpu
from jax.sharding import Mesh, PartitionSpec as P

BF = jnp.bfloat16
F32 = jnp.float32
AXES = ("xlo", "z", "core", "xhi", "y")
QUAD = ("xlo", "core")
PLANE = ("xhi", "y", "xlo", "core")
DP = ("xlo", "z", "core")
WIDTH = 128
PAIR = 256
TOK = 256
SLAB = 1024
STEP = 9


def dot(left, right, left_dim, right_dim):
    return lax.dot_general(
        left, right, (((left_dim,), (right_dim,)), ((), ())), preferred_element_type=F32
    )


def one_hot(shape, test):
    rows = lax.broadcasted_iota(jnp.int32, shape, 0)
    cols = lax.broadcasted_iota(jnp.int32, shape, 1)
    return jnp.where(test(rows, cols), 1.0, 0.0).astype(BF)


def pairs_from_natural():
    return one_hot(
        (PAIR, PAIR),
        lambda r, c: c == ((r >> 1) & 1) * WIDTH + (r >> 2) * 2 + (r & 1),
    )


def natural_from_pairs():
    return one_hot(
        (PAIR, PAIR),
        lambda r, c: r == ((c >> 1) & 1) * WIDTH + (c >> 2) * 2 + (c & 1),
    )


def quads_from_natural():
    return one_hot(
        (PAIR, PAIR),
        lambda r, c: c == ((r >> 2) & 1) * WIDTH + (r >> 3) * 4 + (r & 3),
    )


def device_at(place):
    return place & 1, (((place >> 1) & 15) * STEP) & 15, place >> 5


def place_of(device):
    return (device & 1) * 32 + (((device >> 1) & 15) * STEP & 15) * 2 + (device >> 5)


def device_index(place):
    xlo, zed, core = device_at(place)
    return xlo * 32 + zed * 2 + core


def group_rows(group):
    return one_hot(
        (PAIR, 2 * PAIR), lambda r, c: c == place_of(r >> 2) * 8 + group * 4 + (r & 3)
    )


def owner_rows(group):
    return one_hot(
        (2 * PAIR, PAIR),
        lambda r, c: (((r >> 2) & 1) == group) & (c == device_index(r >> 3) * 4 + (r & 3)),
    )


def expand(factor):
    rows = lax.broadcasted_iota(jnp.int32, factor.shape, 0)
    first = ((rows >> 1) & 1) == 0
    zero = jnp.zeros_like(factor)
    return jnp.concatenate(
        [jnp.where(first, factor, zero), jnp.where(first, zero, factor)], axis=1
    )


def own_block(full):
    rows = lax.broadcasted_iota(jnp.int32, (PAIR, WIDTH), 0)
    return jnp.where(((rows >> 1) & 1) == 0, full[:, :WIDTH], full[:, WIDTH:])


def factor_of(rows, index):
    return expand(rows[:, index * WIDTH : (index + 1) * WIDTH])


def share_kernel(*refs):
    factor_refs, (share_ref, rows_ref, sems) = refs[:6], refs[6:]
    copies = [
        pltpu.make_async_copy(ref, rows_ref.at[at], sems.at[at])
        for at, ref in enumerate(factor_refs)
    ]
    for copy in copies:
        copy.start()
    for copy in copies:
        copy.wait()
    slabs = {}
    for place in range(0, 64, 2):
        quads = tuple(device_at(at)[0] * 2 + device_at(at)[2] for at in (place, place + 1))
        if quads not in slabs:
            thirds = []
            for third in range(3):
                rows = [
                    rows_ref[group * 3 + third, quad * 2 + k].astype(F32)
                    for quad in quads
                    for group in range(2)
                    for k in range(2)
                ]
                thirds.append(jnp.concatenate(rows, axis=0).astype(BF))
            slabs[quads] = jnp.concatenate(thirds, axis=1)
        share_ref[place * 8 : place * 8 + 16, :] = slabs[quads]


def cut_piece(quad_ref, tok_ref, cot_ref, hop, ref):
    cols = pl.ds(pl.multiple_of((quad_ref[0] ^ hop) * PAIR, PAIR), PAIR)
    ref[:TOK, :] = tok_ref[:, cols]
    ref[TOK:, :] = cot_ref[:, cols]


def far_kernel(quad_ref, tok_ref, cot_ref, two_ref, three_ref, sems):
    copies = []
    for at, ref in enumerate((two_ref, three_ref)):
        cols = pl.ds(pl.multiple_of((quad_ref[0] ^ (2 + at)) * PAIR, PAIR), PAIR)
        for which, source in enumerate((tok_ref, cot_ref)):
            copies.append(
                pltpu.make_async_copy(
                    source.at[:, cols],
                    ref.at[which * TOK : (which + 1) * TOK, :],
                    sems.at[2 * at + which],
                )
            )
    for copy in copies:
        copy.start()
    for copy in copies:
        copy.wait()


def near_kernel(quad_ref, tok_ref, cot_ref, after_ref, own_ref, one_ref, *order_refs):
    del after_ref
    cut_piece(quad_ref, tok_ref, cot_ref, 0, own_ref)
    cut_piece(quad_ref, tok_ref, cot_ref, 1, one_ref)
    pairs_ref, quads_ref, first_ref, second_ref = order_refs
    pairs_ref[...] = pairs_from_natural()
    quads_ref[...] = quads_from_natural()
    first_ref[...] = owner_rows(0)
    second_ref[...] = owner_rows(1)


def first_kernel(quad_ref, share_ref, *refs):
    piece_refs, (quads_ref, send_ref, weights_ref) = refs[:4], refs[4:]
    share, nat, quads = share_ref[...], natural_from_pairs(), quads_ref[...]
    weights = jnp.concatenate(
        [dot(group_rows(0), share, 1, 0), dot(group_rows(1), share, 1, 0)], axis=1
    ).astype(BF)
    weights_ref[...] = weights
    gate = dot(quads, dot(nat, factor_of(weights, 0), 1, 0).astype(BF), 1, 1).astype(BF)
    value = dot(quads, dot(nat, factor_of(weights, 1), 1, 0).astype(BF), 1, 1).astype(BF)
    down = factor_of(weights, 2)
    tok = jnp.concatenate([ref[:TOK, :] for ref in piece_refs], axis=0)
    cot = jnp.concatenate([ref[TOK:, :] for ref in piece_refs], axis=0)
    first = dot(jnp.concatenate([gate, value], axis=0), tok, 1, 1).astype(BF)
    back = dot(down, cot, 1, 1).astype(BF)
    for hop in range(4):
        at = pl.multiple_of((quad_ref[0] ^ hop) * TOK, TOK)
        cols = slice(hop * TOK, (hop + 1) * TOK)
        send_ref[:, pl.ds(at, TOK)] = first[:PAIR, cols]
        send_ref[:, pl.ds(SLAB + at, TOK)] = first[PAIR:, cols]
        send_ref[:, pl.ds(2 * SLAB + at, TOK)] = back[:, cols]


def middle_kernel(
    weights_ref,
    recv_ref,
    pairs_ref,
    quads_ref,
    send_ref,
    grad_ref,
    hid_ref,
    gate_ref,
    value_ref,
):
    pairs, quads = pairs_ref[...], quads_ref[...]
    weights = weights_ref[...]
    gate_w = factor_of(weights, 3)
    value_w = factor_of(weights, 4)
    down_w = factor_of(weights, 5)
    gate_fwd = dot(pairs, gate_w, 1, 1).astype(BF)
    value_fwd = dot(pairs, value_w, 1, 1).astype(BF)
    gate_bwd = dot(gate_w, pairs, 1, 1).astype(BF)
    value_bwd = dot(value_w, pairs, 1, 1).astype(BF)
    down_fwd = dot(quads, down_w, 1, 1).astype(BF)
    down_bwd = dot(down_w, quads, 1, 1).astype(BF)
    gate_pre = dot(gate_fwd, recv_ref[:, :SLAB], 1, 0)
    value_pre = dot(value_fwd, recv_ref[:, SLAB : 2 * SLAB], 1, 0)
    sigma = jax.nn.sigmoid(gate_pre)
    hidden = (gate_pre * sigma * value_pre).astype(BF)
    hid_ref[...] = hidden
    send_ref[:, :SLAB] = dot(down_fwd, hidden, 1, 0).astype(BF)
    back = dot(down_bwd, recv_ref[:, 2 * SLAB :], 1, 0)
    gate_back = (back * value_pre * sigma * (1.0 + gate_pre * (1.0 - sigma))).astype(BF)
    value_back = (back * gate_pre * sigma).astype(BF)
    gate_ref[...] = gate_back
    value_ref[...] = value_back
    send_ref[:, SLAB : 2 * SLAB] = dot(gate_bwd, gate_back, 1, 0).astype(BF)
    send_ref[:, 2 * SLAB :] = dot(value_bwd, value_back, 1, 0).astype(BF)
    gate_grad = dot(recv_ref[:, :SLAB], gate_ref[...], 1, 1).astype(BF)
    value_grad = dot(recv_ref[:, SLAB : 2 * SLAB], value_ref[...], 1, 1).astype(BF)
    down_grad = dot(hid_ref[...], recv_ref[:, 2 * SLAB :], 1, 1).astype(BF)
    grad_ref[:, :WIDTH] = own_block(dot(gate_grad, pairs, 1, 0)).astype(BF)
    grad_ref[:, WIDTH : 2 * WIDTH] = own_block(dot(value_grad, pairs, 1, 0)).astype(BF)
    grad_ref[:, 2 * WIDTH :] = own_block(dot(down_grad, quads, 1, 0)).astype(BF)


def inner_kernel(quad_ref, *refs):
    piece_refs, (recv_ref, outer_ref, pairs_ref, quads_ref, first_ref, second_ref, grad_ref) = (
        refs[:4],
        refs[4:],
    )
    pairs, quads = pairs_ref[...], quads_ref[...]
    tok = jnp.concatenate([ref[:TOK, :] for ref in piece_refs], axis=0)
    cot = jnp.concatenate([ref[TOK:, :] for ref in piece_refs], axis=0)

    def columns(first):
        at = [first + pl.multiple_of((quad_ref[0] ^ hop) * TOK, TOK) for hop in range(4)]
        return jnp.concatenate([recv_ref[:, pl.ds(start, TOK)] for start in at], axis=1)

    both = dot(jnp.concatenate([columns(SLAB), columns(2 * SLAB)], axis=0), tok, 1, 0)
    down_grad = dot(columns(0), cot, 1, 0)
    both = dot(pairs, both.astype(BF), 1, 1).astype(BF)
    gate_grad, value_grad = both[:, :PAIR], both[:, PAIR:]
    inner = jnp.concatenate(
        [
            own_block(dot(gate_grad, quads, 1, 0)).astype(BF),
            own_block(dot(value_grad, quads, 1, 0)).astype(BF),
            own_block(down_grad).astype(BF),
        ],
        axis=1,
    )
    grad_ref[...] = (
        dot(first_ref[...], outer_ref[...], 1, 0) + dot(second_ref[...], inner, 1, 0)
    ).astype(BF)


def output_kernel(hops, quad_ref, weights_ref, recv_ref, *refs):
    out_refs = refs[-2:]
    nat = natural_from_pairs()
    quads = quads_from_natural()
    weights = weights_ref[...]
    down = factor_of(weights, 2)
    gate = dot(nat, dot(factor_of(weights, 0), quads, 1, 1).astype(BF), 1, 0).astype(BF)
    value = dot(nat, dot(factor_of(weights, 1), quads, 1, 1).astype(BF), 1, 0).astype(BF)
    quad = quad_ref[0]
    for hop, out_ref in zip(hops, out_refs):
        at = pl.multiple_of((quad ^ hop) * TOK, TOK)
        mixed = dot(recv_ref[:, pl.ds(at, TOK)], down, 0, 0)
        out_ref[:TOK, :] = mixed.astype(BF)
        back = dot(gate, recv_ref[:, pl.ds(SLAB + at, TOK)], 1, 0) + dot(
            value, recv_ref[:, pl.ds(2 * SLAB + at, TOK)], 1, 0
        )
        out_ref[TOK:, :] = back.T.astype(BF)


def place_kernel(quad_ref, own_ref, one_ref, two_ref, three_ref, mixed_ref, back_ref):
    for hop, ref in enumerate((own_ref, one_ref, two_ref, three_ref)):
        at = pl.multiple_of((quad_ref[0] ^ hop) * PAIR, PAIR)
        mixed_ref[:, pl.ds(at, PAIR)] = ref[:TOK, :]
        back_ref[:, pl.ds(at, PAIR)] = ref[TOK:, :]


def end_kernel(scale, grads_ref, *grad_refs):
    def test(r, c):
        xlo, _, core = device_at(c >> 3)
        return r == ((c >> 2) & 1) * 16 + xlo * 8 + core * 4 + (c & 3)

    total = dot(one_hot((32, 2 * PAIR), test), grads_ref[...], 1, 0) * scale
    for group in range(2):
        for third in range(3):
            for block in range(8):
                row = group * 16 + block * 2
                grad_refs[group * 3 + third][block] = total[
                    row : row + 2, third * WIDTH : (third + 1) * WIDTH
                ]


def call(kernel, name, outs, scratch=(), room=40, **specs):
    return pl.pallas_call(
        kernel,
        out_shape=outs,
        scratch_shapes=list(scratch),
        compiler_params=pltpu.CompilerParams(vmem_limit_bytes=room * 1024 * 1024),
        name=name,
        **specs,
    )


def scalar_first(arrays):
    vmem = pl.BlockSpec(memory_space=pltpu.VMEM)
    return [pl.BlockSpec(memory_space=pltpu.SMEM)] + [vmem] * arrays


def exchange(rows):
    order = [[device_index(place) for place in range(64)]]
    return lax.all_to_all(
        rows, DP, split_axis=0, concat_axis=0, axis_index_groups=order, tiled=True
    )


def swap(part, hop):
    return lax.ppermute(part, QUAD, [(at, at ^ hop) for at in range(4)])


def shape(dims, kind=BF):
    return jax.ShapeDtypeStruct(dims, kind)


def local(
    tokens, cotangent, gate_inner, gate_outer, value_inner, value_outer, down_inner, down_outer
):
    scale = float(tokens.shape[0] * lax.axis_size(DP)) ** (-0.5)

    quad = jnp.reshape(lax.axis_index(QUAD), (1,))
    piece, share = shape((2 * TOK, PAIR)), shape((2 * PAIR, 3 * WIDTH))
    shares = call(
        share_kernel,
        "share",
        share,
        [pltpu.VMEM((6, 8, 2, WIDTH), BF), pltpu.SemaphoreType.DMA((6,))],
        room=60,
        in_specs=[pl.BlockSpec(memory_space=pl.ANY)] * 6,
    )(gate_inner, value_inner, down_outer, gate_outer, value_outer, down_inner)
    shares = exchange(shares)
    anywhere = pl.BlockSpec(memory_space=pl.ANY)
    two, three = call(
        far_kernel,
        "far",
        (piece,) * 2,
        [pltpu.SemaphoreType.DMA((4,))],
        room=60,
        in_specs=scalar_first(0) + [anywhere] * 2,
    )(quad, tokens, cotangent)
    square, tall = shape((PAIR, PAIR)), shape((2 * PAIR, PAIR))
    after = [anywhere]
    own, one, pairs, quads, *owners = call(
        near_kernel,
        "near",
        (piece, piece, square, square, tall, tall),
        in_specs=scalar_first(2) + after,
    )(quad, tokens, cotangent, two)
    pieces = (own, swap(one, 1), swap(two, 2), swap(three, 3))

    wide, slab = shape((PAIR, 3 * SLAB)), pltpu.VMEM((PAIR, SLAB), BF)
    send, weights = call(
        first_kernel, "first", (wide, shape((PAIR, 6 * WIDTH))), in_specs=scalar_first(6)
    )(quad, shares, *pieces, quads)
    recv = lax.all_to_all(send, PLANE, split_axis=0, concat_axis=0, tiled=True)
    send, outer = call(middle_kernel, "middle", (wide, shape((PAIR, 3 * WIDTH))), [slab] * 3)(
        weights, recv, pairs, quads
    )
    recv = lax.all_to_all(send, PLANE, split_axis=0, concat_axis=0, tiled=True)
    grads = call(inner_kernel, "inner", share, in_specs=scalar_first(10))(
        quad, *pieces, recv, outer, pairs, quads, *owners
    )
    grads = exchange(grads)
    two, three = call(
        functools.partial(output_kernel, (2, 3)), "output", (piece,) * 2, in_specs=scalar_first(2)
    )(quad, weights, recv)
    three = swap(three, 3)
    own, one = call(
        functools.partial(output_kernel, (0, 1)),
        "output2",
        (piece,) * 2,
        in_specs=scalar_first(2) + after,
    )(quad, weights, recv, three)
    mixed, back = call(
        place_kernel, "place", (shape((TOK, 4 * PAIR)),) * 2, in_specs=scalar_first(4)
    )(quad, own, swap(one, 1), swap(two, 2), three)
    g_gate_o, g_value_o, g_down_i, g_gate_i, g_value_i, g_down_o = call(
        functools.partial(end_kernel, scale), "end", (shape((8, 2, WIDTH), F32),) * 6
    )(grads)
    return mixed, back, g_gate_i, g_gate_o, g_value_i, g_value_o, g_down_i, g_down_o


def solution(mesh):
    fine = Mesh(mesh.devices.reshape(2, 16, 2, 2, 4), AXES)
    rows = P(DP, ("xhi", "y"))
    factor = P(("xhi", "y"), DP, None)
    return jax.shard_map(
        local,
        mesh=fine,
        in_specs=(rows,) * 2 + (factor,) * 6,
        out_specs=(rows,) * 2 + (factor,) * 6,
        check_vma=False,
    )
```
